256 devices in a mesh: cols: 128 (over x_lo, z, y, core), lev: 2 (over x_hi).
Axes of the slice: x: 4 (x_hi: 2, x_lo: 2; x = x_hi * 2 + x_lo), y: 4, z: 8, core: 2. Of those that a mesh axis runs over, the one named last changes fastest.
Arguments:
- u_adj: float32 [128, 128, 16, 128], P('lev', 'cols'), may hold values from -6 to 6
- v_adj: float32 [128, 128, 16, 128], P('lev', 'cols'), may hold values from -6 to 6
- w_adj: float32 [128, 128, 16, 128], P('lev', 'cols'), may hold values from -6 to 6
- theta_adj: float32 [128, 128, 16, 128], P('lev', 'cols'), may hold values from -6 to 6
- p_adj: float32 [128, 128, 16, 128], P('lev', 'cols'), may hold values from -6 to 6
- grad_coef: float32 [128, 128, 16, 128], P('lev', 'cols'), may hold values from 0.3 to 1.2
- squeeze_coef: float32 [128, 128, 16, 128], P('lev', 'cols'), may hold values from 0.3 to 1.2
- wind_first: float32 [128, 128, 16, 128], P('lev', 'cols'), may hold values from -1 to 1
- wind_second: float32 [128, 128, 16, 128], P('lev', 'cols'), may hold values from -1 to 1
- acoustic_inverse: float32 [256, 256], replicated, may hold values from -0.375 to 0.375
Outputs:
- u_out: float32 [128, 128, 16, 128], P('lev', 'cols')
- v_out: float32 [128, 128, 16, 128], P('lev', 'cols')
- w_out: float32 [128, 128, 16, 128], P('lev', 'cols')
- theta_out: float32 [128, 128, 16, 128], P('lev', 'cols')
- p_out: float32 [128, 128, 16, 128], P('lev', 'cols')
The draws below stay inside these ranges and needn't reach their ends.
All inputs are finite; a program needn't handle non-finite values.
Results may differ from the reference program's by a relative error of at most 0.000071.
Values sent between devices are 32-bit elements; how exact they have to be, the bound alone decides.
No kernel may reach another device: no remote copies, remote signals or barrier semaphores. Data moves between devices by JAX's collectives and lax.ppermute only.
A program may use at most 64 MiB of HBM per device.

```python
import math
import jax
import jax.numpy as jnp
from jax import lax

L = 128
PX = 16
PY = 128
TW = 4
TILES = 128


def levels(own_key, dims, pieces, smallest, high):
    def one(axis_at, parts):
        heights = jax.random.uniform(jax.random.fold_in(jax.random.fold_in(own_key, 6), axis_at), (parts,), jnp.float32, smallest / len(pieces), high / len(pieces))
        return jnp.repeat(jnp.exp(heights), dims[axis_at] // parts).reshape((-1,) + (1,) * (len(dims) - axis_at - 1))

    level = one(*pieces[0])
    for cut in pieces[1:]:
        level = level * one(*cut)
    return level


def bell_draw(stream_key, shape, spread, most, split=(), kind=jnp.bfloat16):
    array = spread * jax.random.normal(stream_key, shape, jnp.float32)
    if split:
        array = array * levels(stream_key, shape, split, -0.22, 0.18)
    return jnp.clip(array, -most, most).astype(kind)


def setup_inputs(seed: int = 0) -> dict:
    key_of = jax.random.split(jax.random.key(seed), 11)
    u_adj = bell_draw(key_of[0], (L, TILES, PX, PY), 1.0, 6.0, ((0, 2), (1, 128)), jnp.float32)
    v_adj = bell_draw(key_of[1], (L, TILES, PX, PY), 1.0, 6.0, ((0, 2), (1, 128)), jnp.float32)
    w_adj = bell_draw(key_of[2], (L, TILES, PX, PY), 1.0, 6.0, ((0, 2), (1, 128)), jnp.float32)
    theta_adj = bell_draw(key_of[3], (L, TILES, PX, PY), 1.0, 6.0, ((0, 2), (1, 128)), jnp.float32)
    p_adj = bell_draw(key_of[4], (L, TILES, PX, PY), 1.0, 6.0, ((0, 2), (1, 128)), jnp.float32)
    grad_coef = jnp.clip(jnp.exp(math.log(1.2) - 1.3862944 * jax.random.uniform(key_of[5], (L, TILES, PX, PY), jnp.float32) ** levels(key_of[5], (L, TILES, PX, PY), ((0, 2), (1, 128)), -0.2, 0.2)), 0.3, 1.2)
    squeeze_coef = jnp.clip(jnp.exp(math.log(1.2) - 1.3862944 * jax.random.uniform(key_of[6], (L, TILES, PX, PY), jnp.float32) ** levels(key_of[6], (L, TILES, PX, PY), ((0, 2), (1, 128)), -0.2, 0.2)), 0.3, 1.2)
    wind_first = jnp.clip(jax.random.uniform(key_of[7], (L, TILES, PX, PY), jnp.float32, -1.0, 1.0) * levels(key_of[7], (L, TILES, PX, PY), ((0, 2), (1, 128)), -0.4, 0.0), -1.0, 1.0)
    wind_second = jnp.clip(jax.random.uniform(key_of[8], (L, TILES, PX, PY), jnp.float32, -1.0, 1.0) * levels(key_of[8], (L, TILES, PX, PY), ((0, 2), (1, 128)), -0.4, 0.0), -1.0, 1.0)
    acoustic_inverse = bell_draw(key_of[9], (2 * L, 2 * L), (2 * L) ** -0.5, 0.375, (), jnp.float32)
    return dict(u_adj=u_adj, v_adj=v_adj, w_adj=w_adj, theta_adj=theta_adj, p_adj=p_adj, grad_coef=grad_coef, squeeze_coef=squeeze_coef, wind_first=wind_first, wind_second=wind_second, acoustic_inverse=acoustic_inverse)


def widen_first(field):
    before = jnp.roll(field, TW, axis=-3)[..., -2:, :]
    after = jnp.roll(field, -TW, axis=-3)[..., :2, :]
    return jnp.concatenate([before, field, after], axis=-2)


def widen_second(field):
    before = jnp.roll(field, 1, axis=-3)[..., -2:]
    after = jnp.roll(field, -1, axis=-3)[..., :2]
    return jnp.concatenate([before, field, after], axis=-1)


def slope_first(wide):
    return (8.0 * (wide[..., 3:-1, :] - wide[..., 1:-3, :]) - (wide[..., 4:, :] - wide[..., :-4, :])) / 12.0


def slope_second(wide):
    return (8.0 * (wide[..., 3:-1] - wide[..., 1:-3]) - (wide[..., 4:] - wide[..., :-4])) / 12.0


def reference(u_adj, v_adj, w_adj, theta_adj, p_adj, grad_coef, squeeze_coef, wind_first, wind_second, acoustic_inverse):
    stacked = jnp.concatenate([w_adj.reshape(L, -1), theta_adj.reshape(L, -1)], axis=0)
    solved = jnp.dot(acoustic_inverse.T, stacked, precision=lax.Precision.HIGHEST, preferred_element_type=jnp.float32)
    w_out = solved[:L].reshape(w_adj.shape)
    theta_star = solved[L:].reshape(theta_adj.shape)

    def level(items):
        wind_u, wind_v, press, grad, squeeze, along_first, along_second, star = items
        pressure = squeeze * press
        u_new = wind_u + slope_first(widen_first(pressure))
        v_new = wind_v + slope_second(widen_second(pressure))
        p_new = press + grad * (slope_first(widen_first(wind_u)) + slope_second(widen_second(wind_v)))
        theta_new = star + slope_first(widen_first(along_first * star)) + slope_second(widen_second(along_second * star))
        return u_new, v_new, p_new, theta_new

    u_out, v_out, p_out, theta_out = lax.map(level, (u_adj, v_adj, p_adj, grad_coef, squeeze_coef, wind_first, wind_second, theta_star))
    return (u_out, v_out, w_out, theta_out, p_out)
```

```python
import jax
import jax.numpy as jnp
from jax import lax
from jax.experimental import pallas as pl
from jax.experimental.pallas import tpu as pltpu
from jax.sharding import PartitionSpec as P

TW = 4
f32 = jnp.float32
bf16 = jnp.bfloat16
VMEM = pl.BlockSpec(memory_space=pltpu.VMEM)


def passed_along(array, axis, by):
    devices = lax.axis_size(axis)
    return lax.ppermute(array, axis, [(i, (i + by) % devices) for i in range(devices)])


def split(x):
    high = x.astype(bf16)
    return high, (x - high.astype(f32)).astype(bf16)


def split3(x):
    high = x.astype(bf16)
    rest = x - high.astype(f32)
    middle = rest.astype(bf16)
    return high, middle, (rest - middle.astype(f32)).astype(bf16)


def call(kernel, name, outs, scratch, *args, flops=0):
    shapes = tuple(jax.ShapeDtypeStruct(s, f32) for s in outs)
    size = sum(a.size for a in args) + sum(s.size for s in shapes)
    return pl.pallas_call(
        kernel,
        out_shape=shapes,
        in_specs=[VMEM] * len(args),
        out_specs=(VMEM,) * len(shapes),
        scratch_shapes=scratch,
        name=name,
        cost_estimate=pl.CostEstimate(flops=flops, bytes_accessed=4 * size, transcendentals=0),
        compiler_params=pltpu.CompilerParams(vmem_limit_bytes=32 << 20),
    )(*args)


def row(ref, i, levels, px):
    return ref[pl.ds(i, levels, stride=px), :]


def own_rows_transposed(a_ref, at_ref, me, levels):
    rows = jnp.concatenate(
        [a_ref[pl.ds(me * levels, levels), :], a_ref[pl.ds((2 + me) * levels, levels), :]], axis=0
    )
    at_ref[...] = rows.T


def paired(w_ref, t_ref, i, levels, px):
    halves = []
    for d in range(2):
        x = jnp.concatenate([row(w_ref, i + d, levels, px), row(t_ref, i + d, levels, px)], axis=0)
        halves.append(jnp.concatenate(split(x), axis=0))
    return jnp.concatenate(halves, axis=1)


def left_factor(blocks):
    high, low = split(jnp.concatenate(blocks, axis=0))
    return jnp.concatenate(
        [jnp.concatenate([high, high], axis=1), jnp.concatenate([low, low], axis=1)], axis=0
    )


def solve_first(px, w_ref, t_ref, a_ref, o_ref, at_ref):
    levels = o_ref.shape[1]
    py = o_ref.shape[2]
    me = lax.axis_index("lev")
    own_rows_transposed(a_ref, at_ref, me, levels)
    left = left_factor([at_ref[pl.ds((3 - me) * levels, levels), :]])
    for i in range(0, px, 2):
        r = jnp.dot(left, paired(w_ref, t_ref, i, levels, px), preferred_element_type=f32)
        r = r[:levels] + r[levels:]
        o_ref[i] = r[:, :py]
        o_ref[i + 1] = r[:, py:]


def solve_rest(px, w_ref, t_ref, a_ref, ow_ref, mt_ref, mw_ref, at_ref):
    levels = mt_ref.shape[1]
    py = mt_ref.shape[2]
    me = lax.axis_index("lev")
    own_rows_transposed(a_ref, at_ref, me, levels)
    left = left_factor(
        [
            at_ref[pl.ds((1 - me) * levels, levels), :],
            at_ref[pl.ds((2 + me) * levels, levels), :],
            at_ref[pl.ds(me * levels, levels), :],
        ]
    )
    for i in range(0, px, 2):
        r = jnp.dot(left, paired(w_ref, t_ref, i, levels, px), preferred_element_type=f32)
        r = r[: 3 * levels] + r[3 * levels :]
        for d in range(2):
            part = r[:, d * py : (d + 1) * py]
            ow_ref[pl.ds(i + d, levels, stride=px), :] = part[:levels]
            mt_ref[i + d] = part[levels : 2 * levels]
            mw_ref[pl.ds(i + d, levels, stride=px), :] = part[2 * levels :]


def iota2(shape, dim):
    return lax.broadcasted_iota(jnp.int32, shape, dim)


def rim_selector(py):
    k = iota2((8, py), 0)
    j = iota2((8, py), 1)
    want = jnp.where(k < 2, k, py - 4 + k)
    return jnp.where((j == want) & (k < 4), 1.0, 0.0).astype(bf16)


def rims(field, selector):
    total = 0.0
    for piece in split3(field):
        total = total + lax.dot_general(
            selector, piece, (((1,), (1,)), ((), ())), preferred_element_type=f32
        )
    return total


def pack(px, u_ref, v_ref, p_ref, q_ref, up_ref, down_ref, right_ref, left_ref):
    levels = up_ref.shape[2]
    py = up_ref.shape[3]
    for d in range(2):
        for out, i in ((up_ref, px - 2 + d), (down_ref, d)):
            out[0, d] = row(u_ref, i, levels, px)
            out[1, d] = row(p_ref, i, levels, px) * row(q_ref, i, levels, px)
    selector = rim_selector(py)
    v_rims = rims(v_ref[...], selector)
    p_rims = rims(p_ref[...] * q_ref[...], selector)
    left_ref[0:2] = v_rims[0:2]
    left_ref[2:4] = p_rims[0:2]
    right_ref[0:2] = v_rims[2:4]
    right_ref[2:4] = p_rims[2:4]


def band(py):
    k = iota2((py, py), 0)
    j = iota2((py, py), 1)
    d = k - j
    one = jnp.where(d == 1, 8.0, jnp.where(d == -1, -8.0, 0.0))
    two = jnp.where(d == 2, -1.0, jnp.where(d == -2, 1.0, 0.0))
    return (one + two).astype(bf16)


def rim_band(py):
    k = iota2((4, py), 0)
    j = iota2((4, py), 1)
    d = jnp.where(k < 2, k - 2, py - 2 + k) - j
    one = jnp.where(d == 1, 8.0, jnp.where(d == -1, -8.0, 0.0))
    two = jnp.where(d == 2, -1.0, jnp.where(d == -2, 1.0, 0.0))
    return (one + two).astype(bf16)


def second_slope(field, rim):
    py = field.shape[1]
    center = band(py)
    edge = rim_band(py)
    total = 0.0
    for piece in split(field):
        total = total + jnp.dot(piece, center, preferred_element_type=f32)
    for piece in split(rim):
        total = total + lax.dot_general(
            piece, edge, (((0,), (0,)), ((), ())), preferred_element_type=f32
        )
    return total * (1.0 / 12.0)


def first_slope(rows, i):
    return (8.0 * (rows(i + 1) - rows(i - 1)) - (rows(i + 2) - rows(i - 2))) * (1.0 / 12.0)


def update(px, u_ref, v_ref, p_ref, g_ref, q_ref, before_ref, after_ref, lrim_ref, rrim_ref,
           uo_ref, vo_ref, po_ref, pr_ref, gv_ref):
    levels = before_ref.shape[2]
    pressure = p_ref[...] * q_ref[...]
    pr_ref[...] = pressure
    prim = jnp.concatenate([lrim_ref[2:4], rrim_ref[2:4]], axis=0)
    vo_ref[...] = v_ref[...] + second_slope(pressure, prim)
    vrim = jnp.concatenate([lrim_ref[0:2], rrim_ref[0:2]], axis=0)
    gv_ref[...] = second_slope(v_ref[...], vrim)

    def reader(ref, at):
        def rows(i):
            if i < 0:
                return before_ref[at, i + 2]
            if i >= px:
                return after_ref[at, i - px]
            return row(ref, i, levels, px)

        return rows

    u_rows = reader(u_ref, 0)
    p_rows = reader(pr_ref, 1)
    for i in range(px):
        here = pl.ds(i, levels, stride=px)
        uo_ref[here, :] = u_ref[here, :] + first_slope(p_rows, i)
        po_ref[here, :] = p_ref[here, :] + g_ref[here, :] * (
            first_slope(u_rows, i) + gv_ref[here, :]
        )


def theta_pack(px, got_ref, mine_ref, wf_ref, ws_ref, star_ref, up_ref, down_ref, right_ref, left_ref,
               second_ref):
    levels = got_ref.shape[1]
    py = got_ref.shape[2]
    for i in range(px):
        star = got_ref[i] + mine_ref[i]
        star_ref[i] = star
        second_ref[pl.ds(i * levels, levels), :] = row(ws_ref, i, levels, px) * star
        if i < 2:
            down_ref[i] = row(wf_ref, i, levels, px) * star
        if i >= px - 2:
            up_ref[i - px + 2] = row(wf_ref, i, levels, px) * star
    got = rims(second_ref[...], rim_selector(py))
    left_ref[...] = got[0:2]
    right_ref[...] = got[2:4]


def theta_finish(px, star_ref, wf_ref, ws_ref, before_ref, after_ref, lrim_ref, rrim_ref, o_ref,
                 first_ref, second_ref):
    levels = star_ref.shape[1]
    first_ref[0:2] = before_ref[...]
    first_ref[px + 2 :] = after_ref[...]
    for i in range(px):
        star = star_ref[i]
        first_ref[i + 2] = row(wf_ref, i, levels, px) * star
        second_ref[pl.ds(i * levels, levels), :] = row(ws_ref, i, levels, px) * star
    rim = jnp.concatenate([lrim_ref[...], rrim_ref[...]], axis=0)
    second_ref[...] = second_slope(second_ref[...], rim)

    def rows(i):
        return first_ref[i + 2]

    for i in range(px):
        o_ref[pl.ds(i, levels, stride=px), :] = (
            star_ref[i] + first_slope(rows, i) + second_ref[pl.ds(i * levels, levels), :]
        )


def kernel_for(px, body):
    def kernel(*refs):
        body(px, *refs)

    return kernel


def on_device(u, v, w, t, p, grad, squeeze, wind_first, wind_second, a):
    levels, _, px, py = u.shape
    cells = levels * px
    u2, v2, w2, t2, p2, g2, q2, wf2, ws2 = (
        x.reshape(cells, py) for x in (u, v, w, t, p, grad, squeeze, wind_first, wind_second)
    )
    at = pltpu.VMEM((4 * levels, 2 * levels), f32)
    column = (px, levels, py)
    (other_t,) = call(kernel_for(px, solve_first), "solve_first", [column], [at], w2, t2, a)
    got_t = passed_along(other_t, "lev", 1)
    up, down, right, left = call(
        kernel_for(px, pack), "pack",
        [(2, 2, levels, py), (2, 2, levels, py), (4, cells), (4, cells)], [], u2, v2, p2, q2)
    before = passed_along(up, "cols", TW)
    after = passed_along(down, "cols", -TW)
    lrim = passed_along(right, "cols", 1)
    rrim = passed_along(left, "cols", -1)
    other_w, mine_t, mine_w = call(
        kernel_for(px, solve_rest), "solve_rest", [(cells, py), column, (cells, py)], [at], w2, t2, a)
    got_w = passed_along(other_w, "lev", 1)
    u_out, v_out, p_out = call(
        kernel_for(px, update), "update", [(cells, py)] * 3,
        [pltpu.VMEM((cells, py), f32)] * 2, u2, v2, p2, g2, q2, before, after, lrim, rrim)
    star, up, down, right, left = call(
        kernel_for(px, theta_pack), "theta_pack",
        [column, (2, levels, py), (2, levels, py), (2, cells), (2, cells)],
        [pltpu.VMEM((cells, py), f32)], got_t, mine_t, wf2, ws2)
    before = passed_along(up, "cols", TW)
    after = passed_along(down, "cols", -TW)
    lrim = passed_along(right, "cols", 1)
    rrim = passed_along(left, "cols", -1)
    (theta_out,) = call(
        kernel_for(px, theta_finish), "theta_finish", [(cells, py)],
        [pltpu.VMEM((px + 4, levels, py), f32), pltpu.VMEM((cells, py), f32)],
        star, wf2, ws2, before, after, lrim, rrim)
    w_out = mine_w + got_w
    return tuple(x.reshape(u.shape) for x in (u_out, v_out, w_out, theta_out, p_out))


def solution(mesh):
    spread = P("lev", "cols", None, None)
    return jax.shard_map(
        on_device,
        mesh=mesh,
        in_specs=(spread,) * 9 + (P(),),
        out_specs=(spread,) * 5,
        check_vma=False,
    )
```

```python
import jax
import jax.numpy as jnp
from jax import lax
from jax.experimental import pallas as pl
from jax.experimental.pallas import tpu as pltpu
from jax.sharding import PartitionSpec as P

TW = 4
FIRST_LIMIT = (53 << 20) + (640 << 10)
LONG = 12_000_000_000
W_COST = 0
T_COST = 0
F_COST = 0
f32 = jnp.float32
bf16 = jnp.bfloat16
VMEM = pl.BlockSpec(memory_space=pltpu.VMEM)


def passed_along(array, axis, by):
    devices = lax.axis_size(axis)
    return lax.ppermute(array, axis, [(i, (i + by) % devices) for i in range(devices)])


def split(x):
    high = x.astype(bf16)
    return high, (x - high.astype(f32)).astype(bf16)


def split3(x):
    high = x.astype(bf16)
    rest = x - high.astype(f32)
    middle = rest.astype(bf16)
    return high, middle, (rest - middle.astype(f32)).astype(bf16)


HBM = pl.BlockSpec(memory_space=pl.ANY)


def call(kernel, name, outs, scratch, *args, flops=0, in_space=VMEM, out_space=VMEM, limit=32 << 20, after=()):
    shapes = tuple(jax.ShapeDtypeStruct(s, f32) for s in outs)
    size = sum(a.size for a in args) + sum(s.size for s in shapes)

    def body(*refs):
        kernel(*refs[: len(args)], *refs[len(args) + len(after) :])

    return pl.pallas_call(
        body,
        out_shape=shapes,
        in_specs=[in_space] * len(args) + [HBM] * len(after),
        out_specs=out_space if isinstance(out_space, tuple) else (out_space,) * len(shapes),
        scratch_shapes=scratch,
        name=name,
        cost_estimate=pl.CostEstimate(flops=flops, bytes_accessed=4 * size, transcendentals=0),
        compiler_params=pltpu.CompilerParams(vmem_limit_bytes=limit),
    )(*args, *after)


def row(ref, i, levels, px):
    return ref[pl.ds(i, levels, stride=px), :]


def own_rows_transposed(a_ref, at_ref, me, levels):
    rows = jnp.concatenate(
        [a_ref[pl.ds(me * levels, levels), :], a_ref[pl.ds((2 + me) * levels, levels), :]], axis=0
    )
    at_ref[...] = rows.T


def left_factor(blocks):
    high, low = split(jnp.concatenate(blocks, axis=0))
    return jnp.concatenate(
        [jnp.concatenate([high, high], axis=1), jnp.concatenate([low, low], axis=1)], axis=0
    )


def paired(pieces):
    halves = []
    for w_part, t_part in pieces:
        halves.append(jnp.concatenate(split(jnp.concatenate([w_part, t_part], axis=0)), axis=0))
    return jnp.concatenate(halves, axis=1)


def iota2(shape, dim):
    return lax.broadcasted_iota(jnp.int32, shape, dim)


def rim_selector(py):
    k = iota2((8, py), 0)
    j = iota2((8, py), 1)
    want = jnp.where(k < 2, k, py - 4 + k)
    return jnp.where((j == want) & (k < 4), 1.0, 0.0).astype(bf16)


def rims(field, selector):
    total = 0.0
    for piece in split3(field):
        total = total + lax.dot_general(
            selector, piece, (((1,), (1,)), ((), ())), preferred_element_type=f32
        )
    return total


def rim_slot(i, px):
    return i if i < 2 else i - px + 4


def sender(sems):
    copies = []

    def send(source, target):
        copy = pltpu.make_async_copy(source, target, sems.at[len(copies)])
        copy.start()
        copies.append(copy)

    return copies, send


def solve_theta(px, w_hbm, t_hbm, a_hbm, rim_ref, inner_hbm, w_ref, t_ref, a_ref, at_ref, full_ref,
                inner_ref, sems):
    cells, py = w_hbm.shape
    levels = cells // px
    copies, send = sender(sems)
    send(a_hbm, a_ref)
    send(w_hbm, w_ref)
    send(t_hbm, t_ref)
    me = lax.axis_index("lev")
    copies[0].wait()
    own_rows_transposed(a_ref, at_ref, me, levels)
    left = left_factor([at_ref[pl.ds((3 - me) * levels, levels), :]])
    copies[1].wait()
    copies[2].wait()
    for i in [*range(2, px - 2, 2), 0, px - 2]:
        if i == 0:
            send(inner_ref, inner_hbm)
        right = paired([(row(w_ref, i + d, levels, px), row(t_ref, i + d, levels, px)) for d in range(2)])
        r = jnp.dot(left, right, preferred_element_type=f32)
        r = r[:levels] + r[levels:]
        for d in range(2):
            part = r[:, d * py : (d + 1) * py]
            full_ref[pl.ds(i + d, levels, stride=px), :] = part
            if 2 <= i < px - 2:
                inner_ref[i + d - 2] = part
            else:
                rim_ref[pl.ds(rim_slot(i + d, px) * levels, levels), :] = part
    edges = rims(full_ref[...], rim_selector(py))
    for k in range(levels * px // py):
        rim_ref[pl.ds(4 * levels + 4 * k, 4), :] = edges[0:4, k * py : (k + 1) * py]
    copies[3].wait()


def solve_rest(px, w_ref, t_ref, a_ref, ow_ref, mw_ref, mt_ref, at_ref):
    levels = w_ref.shape[0] // px
    py = w_ref.shape[1]
    me = lax.axis_index("lev")
    own_rows_transposed(a_ref, at_ref, me, levels)
    left = left_factor(
        [
            at_ref[pl.ds((1 - me) * levels, levels), :],
            at_ref[pl.ds(me * levels, levels), :],
            at_ref[pl.ds((2 + me) * levels, levels), :],
        ]
    )
    for i in range(0, px, 2):
        right = paired([(row(w_ref, i + d, levels, px), row(t_ref, i + d, levels, px)) for d in range(2)])
        r = jnp.dot(left, right, preferred_element_type=f32)
        r = r[: 3 * levels] + r[3 * levels :]
        for d in range(2):
            part = r[:, d * py : (d + 1) * py]
            here = pl.ds(i + d, levels, stride=px)
            ow_ref[here, :] = part[:levels]
            mw_ref[here, :] = part[levels : 2 * levels]
            mt_ref[here, :] = part[2 * levels :]


def pack_rows(px, first, u_ref, p_ref, q_ref, wf_ref, mt_ref, got_ref, out):
    levels = out.shape[2]
    start = (1 - first) * (px - 2)
    for d in range(2):
        i = start + d
        out[0, d] = row(u_ref, i, levels, px)
        out[1, d] = row(p_ref, i, levels, px) * row(q_ref, i, levels, px)
        star = row(mt_ref, i, levels, px) + got_ref[pl.ds(((1 - first) * 2 + d) * levels, levels), :]
        out[2, d] = row(wf_ref, i, levels, px) * star


def pack_even(px, u_ref, p_ref, q_ref, wf_ref, mt_ref, got_ref, e4_ref):
    odd4 = lax.rem(lax.div(lax.axis_index("cols"), TW), 2)
    pack_rows(px, odd4, u_ref, p_ref, q_ref, wf_ref, mt_ref, got_ref, e4_ref)


def pack(px, u_ref, v_ref, p_ref, q_ref, wf_ref, ws_ref, mt_ref, got_ref, o4_ref, e1_ref, o1_ref):
    levels = o4_ref.shape[2]
    py = o4_ref.shape[3]
    cols = lax.axis_index("cols")
    odd4 = lax.rem(lax.div(cols, TW), 2)
    odd1 = lax.rem(cols, 2)
    pack_rows(px, 1 - odd4, u_ref, p_ref, q_ref, wf_ref, mt_ref, got_ref, o4_ref)
    selector = rim_selector(py)
    got_rims = jnp.concatenate(
        [got_ref[pl.ds(4 * levels + 4 * k, 4), :] for k in range(levels * px // py)], axis=1
    )
    v_rims = rims(v_ref[...], selector)[0:4]
    p_rims = rims(p_ref[...] * q_ref[...], selector)[0:4]
    t_rims = rims(ws_ref[...], selector)[0:4] * (rims(mt_ref[...], selector)[0:4] + got_rims)
    first = jnp.concatenate([v_rims[0:2], p_rims[0:2], t_rims[0:2], t_rims[0:2]], axis=0)
    last = jnp.concatenate([v_rims[2:4], p_rims[2:4], t_rims[2:4], t_rims[2:4]], axis=0)
    is_odd = odd1 == 1
    e1_ref[...] = jnp.where(is_odd, first, last)
    o1_ref[...] = jnp.where(is_odd, last, first)


def band(py):
    k = iota2((py, py), 0)
    j = iota2((py, py), 1)
    d = k - j
    one = jnp.where(d == 1, 8.0, jnp.where(d == -1, -8.0, 0.0))
    two = jnp.where(d == 2, -1.0, jnp.where(d == -2, 1.0, 0.0))
    return (one + two).astype(bf16)


def rim_band(py):
    k = iota2((4, py), 0)
    j = iota2((4, py), 1)
    d = jnp.where(k < 2, k - 2, py - 2 + k) - j
    one = jnp.where(d == 1, 8.0, jnp.where(d == -1, -8.0, 0.0))
    two = jnp.where(d == 2, -1.0, jnp.where(d == -2, 1.0, 0.0))
    return (one + two).astype(bf16)


def second_inner(field):
    center = band(field.shape[1])
    total = 0.0
    for piece in split(field):
        total = total + jnp.dot(piece, center, preferred_element_type=f32)
    return total * (1.0 / 12.0)


def second_rim(rim, py):
    edge = rim_band(py)
    total = 0.0
    for piece in split(rim):
        total = total + lax.dot_general(
            piece, edge, (((0,), (0,)), ((), ())), preferred_element_type=f32
        )
    return total * (1.0 / 12.0)


def first_inner(rows, i, px):
    one = rows(i + 1) if i + 1 < px else 0.0
    one = one - rows(i - 1) if i >= 1 else one
    two = rows(i + 2) if i + 2 < px else 0.0
    two = two - rows(i - 2) if i >= 2 else two
    return (8.0 * one - two) * (1.0 / 12.0)


def first_rim(i, before, after, px):
    if i == 0:
        return (before[0] - 8.0 * before[1]) * (1.0 / 12.0)
    if i == 1:
        return before[1] * (1.0 / 12.0)
    if i == px - 2:
        return after[0] * (-1.0 / 12.0)
    return (8.0 * after[0] - after[1]) * (1.0 / 12.0)


def first_inner(rows, i, px):
    one = rows(i + 1) if i + 1 < px else 0.0
    one = one - rows(i - 1) if i >= 1 else one
    two = rows(i + 2) if i + 2 < px else 0.0
    two = two - rows(i - 2) if i >= 2 else two
    return (8.0 * one - two) * (1.0 / 12.0)


def first_rim(i, before, after, px):
    if i == 0:
        return (before[0] - 8.0 * before[1]) * (1.0 / 12.0)
    if i == 1:
        return before[1] * (1.0 / 12.0)
    if i == px - 2:
        return after[0] * (-1.0 / 12.0)
    return (8.0 * after[0] - after[1]) * (1.0 / 12.0)


def winds_inner(px, u_ref, v_ref, p_ref, g_ref, q_ref, uo_ref, vo_ref, po_ref, pr_ref, gv_ref):
    levels = u_ref.shape[0] // px
    pressure = p_ref[...] * q_ref[...]
    pr_ref[...] = pressure
    vo_ref[...] = v_ref[...] + second_inner(pressure)
    gv_ref[...] = second_inner(v_ref[...])

    def u_rows(i):
        return row(u_ref, i, levels, px)

    def p_rows(i):
        return row(pr_ref, i, levels, px)

    for i in range(px):
        here = pl.ds(i, levels, stride=px)
        uo_ref[here, :] = u_ref[here, :] + first_inner(p_rows, i, px)
        po_ref[here, :] = p_ref[here, :] + g_ref[here, :] * (
            first_inner(u_rows, i, px) + gv_ref[here, :]
        )


def theta_inner(px, rim_ref, inner_ref, mt_ref, wf_ref, ws_ref, o_ref, star_ref, first_ref):
    levels = inner_ref.shape[1]
    for i in range(px):
        if 2 <= i < px - 2:
            got = inner_ref[i - 2]
        else:
            got = rim_ref[pl.ds(rim_slot(i, px) * levels, levels), :]
        star = got + row(mt_ref, i, levels, px)
        star_ref[pl.ds(i, levels, stride=px), :] = star
        first_ref[i] = row(wf_ref, i, levels, px) * star
    star = star_ref[...]
    star_ref[...] = star + second_inner(ws_ref[...] * star)

    def rows(i):
        return first_ref[i]

    for i in range(px):
        here = pl.ds(i, levels, stride=px)
        o_ref[here, :] = star_ref[here, :] + first_inner(rows, i, px)


def halo_rows(e4_ref, o4_ref, at, odd):
    before = [jnp.where(odd, e4_ref[at, d], o4_ref[at, d]) for d in range(2)]
    after = [jnp.where(odd, o4_ref[at, d], e4_ref[at, d]) for d in range(2)]
    return before, after


def halo_columns(e1_ref, o1_ref, at, odd):
    e1 = e1_ref[2 * at : 2 * at + 2]
    o1 = o1_ref[2 * at : 2 * at + 2]
    return jnp.concatenate([jnp.where(odd, e1, o1), jnp.where(odd, o1, e1)], axis=0)


def parities():
    cols = lax.axis_index("cols")
    return lax.rem(lax.div(cols, TW), 2) == 1, lax.rem(cols, 2) == 1


def finish(px, ub_ref, vb_ref, pb_ref, g_ref, tb_ref, e4_ref, o4_ref, e1_ref, o1_ref,
           u_hbm, v_hbm, t_hbm, p_hbm, u_ref, v_ref, t_ref, p_ref, sems):
    cells, py = ub_ref.shape
    levels = cells // px
    odd4, odd1 = parities()
    copies, send = sender(sems)
    edge_rows = (0, 1, px - 2, px - 1)
    u_ref[...] = ub_ref[...]
    before, after = halo_rows(e4_ref, o4_ref, 1, odd4)
    for i in edge_rows:
        here = pl.ds(i, levels, stride=px)
        u_ref[here, :] = ub_ref[here, :] + first_rim(i, before, after, px)
    send(u_ref, u_hbm)
    v_ref[...] = vb_ref[...] + second_rim(halo_columns(e1_ref, o1_ref, 1, odd1), py)
    send(v_ref, v_hbm)
    t_ref[...] = tb_ref[...] + second_rim(halo_columns(e1_ref, o1_ref, 2, odd1), py)
    before, after = halo_rows(e4_ref, o4_ref, 2, odd4)
    for i in edge_rows:
        here = pl.ds(i, levels, stride=px)
        t_ref[here, :] = t_ref[here, :] + first_rim(i, before, after, px)
    send(t_ref, t_hbm)
    p_ref[...] = pb_ref[...] + g_ref[...] * second_rim(halo_columns(e1_ref, o1_ref, 0, odd1), py)
    before, after = halo_rows(e4_ref, o4_ref, 0, odd4)
    for i in edge_rows:
        here = pl.ds(i, levels, stride=px)
        p_ref[here, :] = p_ref[here, :] + g_ref[here, :] * first_rim(i, before, after, px)
    send(p_ref, p_hbm)
    for copy in copies:
        copy.wait()


def kernel_for(px, body):
    def kernel(*refs):
        body(px, *refs)

    return kernel


def exchange(array, step, odd_pairs):
    devices = lax.axis_size("cols")
    pairs = []
    for c in range(devices):
        up = ((c // step) % 2 == 1) == odd_pairs
        pairs.append((c, (c + step if up else c - step) % devices))
    return lax.ppermute(array, "cols", pairs)


def on_device(u, v, w, t, p, grad, squeeze, wind_first, wind_second, a):
    levels, _, px, py = u.shape
    cells = levels * px
    u2, v2, w2, t2, p2, g2, q2, wf2, ws2 = (
        x.reshape(cells, py) for x in (u, v, w, t, p, grad, squeeze, wind_first, wind_second)
    )
    at = pltpu.VMEM((4 * levels, 2 * levels), f32)
    flat = (cells, py)
    rim_rows = 4 * levels + 4 * (cells // py)
    rim_shape = (rim_rows, py)
    inner_shape = (px - 4, levels, py)
    rim_t, inner_t = call(
        kernel_for(px, solve_theta), "solve_theta", [rim_shape, inner_shape],
        [pltpu.VMEM(flat, f32), pltpu.VMEM(flat, f32), pltpu.VMEM(a.shape, f32), at,
         pltpu.VMEM(flat, f32), pltpu.VMEM(inner_shape, f32), pltpu.SemaphoreType.DMA((4,))],
        w2, t2, a, in_space=HBM, out_space=(VMEM, HBM), limit=FIRST_LIMIT, flops=LONG)
    got_rim = passed_along(rim_t, "lev", 1)
    got_inner = passed_along(inner_t, "lev", 1)
    other_w, mine_w, mine_t = call(
        kernel_for(px, solve_rest), "solve_rest", [flat] * 3, [at], w2, t2, a, flops=LONG, after=(rim_t,))
    o4, e1, o1 = call(
        kernel_for(px, pack), "pack", [(3, 2, levels, py)] + [(8, cells)] * 2, [],
        u2, v2, p2, q2, wf2, ws2, mine_t, got_rim, flops=LONG, after=(other_w,))
    (e4,) = call(
        kernel_for(px, pack_even), "pack_even", [(3, 2, levels, py)], [],
        u2, p2, q2, wf2, mine_t, got_rim, flops=LONG, after=(o1,))
    got_w = passed_along(other_w, "lev", 1)
    halos = (exchange(e4, TW, False), exchange(o4, TW, True), exchange(e1, 1, False), exchange(o1, 1, True))
    u_in, v_in, p_in = call(
        kernel_for(px, winds_inner), "winds_inner", [flat] * 3, [pltpu.VMEM(flat, f32)] * 2,
        u2, v2, p2, g2, q2, after=(e4,), flops=W_COST)
    (t_in,) = call(
        kernel_for(px, theta_inner), "theta_inner", [flat],
        [pltpu.VMEM(flat, f32), pltpu.VMEM((px, levels, py), f32)],
        got_rim, got_inner, mine_t, wf2, ws2, flops=T_COST)
    w_out = mine_w + got_w
    u_out, v_out, theta_out, p_out = call(
        kernel_for(px, finish), "finish", [flat] * 4,
        [pltpu.VMEM(flat, f32)] * 4 + [pltpu.SemaphoreType.DMA((4,))],
        u_in, v_in, p_in, g2, t_in, *halos, out_space=HBM, flops=F_COST)
    outs = (u_out, v_out, w_out, theta_out, p_out)
    return tuple(x.reshape(u.shape) for x in outs)


def solution(mesh):
    spread = P("lev", "cols", None, None)
    return jax.shard_map(
        on_device,
        mesh=mesh,
        in_specs=(spread,) * 9 + (P(),),
        out_specs=(spread,) * 5,
        check_vma=False,
    )
```

```python
import jax
import jax.numpy as jnp
from jax import lax
from jax.experimental import pallas as pl
from jax.experimental.pallas import tpu as pltpu
from jax.sharding import PartitionSpec as P

TW = 4
FIRST_LIMIT = (53 << 20) + (640 << 10)
LONG = 12_000_000_000
W_COST = 0
I_COST = 0
T_COST = 0
F_COST = 0
f32 = jnp.float32
bf16 = jnp.bfloat16
VMEM = pl.BlockSpec(memory_space=pltpu.VMEM)


def passed_along(array, axis, by):
    devices = lax.axis_size(axis)
    return lax.ppermute(array, axis, [(i, (i + by) % devices) for i in range(devices)])


def split(x):
    high = x.astype(bf16)
    return high, (x - high.astype(f32)).astype(bf16)


def split3(x):
    high = x.astype(bf16)
    rest = x - high.astype(f32)
    middle = rest.astype(bf16)
    return high, middle, (rest - middle.astype(f32)).astype(bf16)


HBM = pl.BlockSpec(memory_space=pl.ANY)


def call(kernel, name, outs, scratch, *args, flops=0, in_space=VMEM, out_space=VMEM, limit=32 << 20, after=()):
    shapes = tuple(jax.ShapeDtypeStruct(s, f32) for s in outs)
    size = sum(a.size for a in args) + sum(s.size for s in shapes)

    def body(*refs):
        kernel(*refs[: len(args)], *refs[len(args) + len(after) :])

    return pl.pallas_call(
        body,
        out_shape=shapes,
        in_specs=[in_space] * len(args) + [HBM] * len(after),
        out_specs=out_space if isinstance(out_space, tuple) else (out_space,) * len(shapes),
        scratch_shapes=scratch,
        name=name,
        cost_estimate=pl.CostEstimate(flops=flops, bytes_accessed=4 * size, transcendentals=0),
        compiler_params=pltpu.CompilerParams(vmem_limit_bytes=limit),
    )(*args, *after)


def row(ref, i, levels, px):
    return ref[pl.ds(i, levels, stride=px), :]


def own_rows_transposed(a_ref, at_ref, me, levels):
    rows = jnp.concatenate(
        [a_ref[pl.ds(me * levels, levels), :], a_ref[pl.ds((2 + me) * levels, levels), :]], axis=0
    )
    at_ref[...] = rows.T


def left_factor(blocks):
    high, low = split(jnp.concatenate(blocks, axis=0))
    return jnp.concatenate(
        [jnp.concatenate([high, high], axis=1), jnp.concatenate([low, low], axis=1)], axis=0
    )


def paired(pieces):
    halves = []
    for w_part, t_part in pieces:
        halves.append(jnp.concatenate(split(jnp.concatenate([w_part, t_part], axis=0)), axis=0))
    return jnp.concatenate(halves, axis=1)


def iota2(shape, dim):
    return lax.broadcasted_iota(jnp.int32, shape, dim)


def rim_selector(py):
    k = iota2((8, py), 0)
    j = iota2((8, py), 1)
    want = jnp.where(k < 2, k, py - 4 + k)
    return jnp.where((j == want) & (k < 4), 1.0, 0.0).astype(bf16)


def rims(field, selector):
    total = 0.0
    for piece in split3(field):
        total = total + lax.dot_general(
            selector, piece, (((1,), (1,)), ((), ())), preferred_element_type=f32
        )
    return total


def rim_slot(i, px):
    return i if i < 2 else i - px + 4


def sender(sems):
    copies = []

    def send(source, target):
        copy = pltpu.make_async_copy(source, target, sems.at[len(copies)])
        copy.start()
        copies.append(copy)

    return copies, send


def solve_rim(px, w_hbm, t_hbm, a_hbm, rim_ref, w_ref, t_ref, a_ref, at_ref, full_ref, sems):
    cells, py = w_hbm.shape
    levels = cells // px
    copies, send = sender(sems)
    send(a_hbm, a_ref)
    send(w_hbm, w_ref)
    send(t_hbm, t_ref)
    me = lax.axis_index("lev")
    copies[0].wait()
    own_rows_transposed(a_ref, at_ref, me, levels)
    left = left_factor([at_ref[pl.ds((3 - me) * levels, levels), :]])
    copies[1].wait()
    copies[2].wait()
    for i, part in solved(px, left, w_ref, t_ref):
        full_ref[pl.ds(i, levels, stride=px), :] = part
        if not 2 <= i < px - 2:
            rim_ref[pl.ds(rim_slot(i, px) * levels, levels), :] = part
    edges = rims(full_ref[...], rim_selector(py))
    for k in range(levels * px // py):
        rim_ref[pl.ds(4 * levels + 4 * k, 4), :] = edges[0:4, k * py : (k + 1) * py]


def solved(px, left, w_ref, t_ref):
    levels = w_ref.shape[0] // px
    py = w_ref.shape[1]
    half = left.shape[0] // 2
    for i in range(0, px, 2):
        right = paired([(row(w_ref, i + d, levels, px), row(t_ref, i + d, levels, px)) for d in range(2)])
        r = jnp.dot(left, right, preferred_element_type=f32)
        r = r[:half] + r[half:]
        yield i, r[:, :py]
        yield i + 1, r[:, py:]


def solve_inner(px, w_ref, t_ref, a_ref, inner_ref, mt_ref, at_ref):
    levels = w_ref.shape[0] // px
    me = lax.axis_index("lev")
    own_rows_transposed(a_ref, at_ref, me, levels)
    left = left_factor([at_ref[pl.ds((3 - me) * levels, levels), :], at_ref[pl.ds((2 + me) * levels, levels), :]])
    for i, part in solved(px, left, w_ref, t_ref):
        if 2 <= i < px - 2:
            inner_ref[i - 2] = part[:levels]
        mt_ref[pl.ds(i, levels, stride=px), :] = part[levels:]


def solve_w(px, w_ref, t_ref, a_ref, ow_ref, mw_ref, at_ref):
    levels = w_ref.shape[0] // px
    me = lax.axis_index("lev")
    own_rows_transposed(a_ref, at_ref, me, levels)
    left = left_factor([at_ref[pl.ds((1 - me) * levels, levels), :], at_ref[pl.ds(me * levels, levels), :]])
    for i, part in solved(px, left, w_ref, t_ref):
        here = pl.ds(i, levels, stride=px)
        ow_ref[here, :] = part[:levels]
        mw_ref[here, :] = part[levels:]


def pack_rows(px, first, u_ref, p_ref, q_ref, wf_ref, mt_ref, got_ref, out):
    levels = out.shape[2]
    start = (1 - first) * (px - 2)
    for d in range(2):
        i = start + d
        out[0, d] = row(u_ref, i, levels, px)
        out[1, d] = row(p_ref, i, levels, px) * row(q_ref, i, levels, px)
        star = row(mt_ref, i, levels, px) + got_ref[pl.ds(((1 - first) * 2 + d) * levels, levels), :]
        out[2, d] = row(wf_ref, i, levels, px) * star


def pack_even(px, u_ref, p_ref, q_ref, wf_ref, mt_ref, got_ref, e4_ref):
    odd4 = lax.rem(lax.div(lax.axis_index("cols"), TW), 2)
    pack_rows(px, odd4, u_ref, p_ref, q_ref, wf_ref, mt_ref, got_ref, e4_ref)


def pack(px, u_ref, v_ref, p_ref, q_ref, wf_ref, ws_ref, mt_ref, got_ref, o4_ref, e1_ref, o1_ref):
    levels = o4_ref.shape[2]
    py = o4_ref.shape[3]
    cols = lax.axis_index("cols")
    odd4 = lax.rem(lax.div(cols, TW), 2)
    odd1 = lax.rem(cols, 2)
    pack_rows(px, 1 - odd4, u_ref, p_ref, q_ref, wf_ref, mt_ref, got_ref, o4_ref)
    selector = rim_selector(py)
    got_rims = jnp.concatenate(
        [got_ref[pl.ds(4 * levels + 4 * k, 4), :] for k in range(levels * px // py)], axis=1
    )
    v_rims = rims(v_ref[...], selector)[0:4]
    p_rims = rims(p_ref[...] * q_ref[...], selector)[0:4]
    t_rims = rims(ws_ref[...], selector)[0:4] * (rims(mt_ref[...], selector)[0:4] + got_rims)
    first = jnp.concatenate([v_rims[0:2], p_rims[0:2], t_rims[0:2], t_rims[0:2]], axis=0)
    last = jnp.concatenate([v_rims[2:4], p_rims[2:4], t_rims[2:4], t_rims[2:4]], axis=0)
    is_odd = odd1 == 1
    e1_ref[...] = jnp.where(is_odd, first, last)
    o1_ref[...] = jnp.where(is_odd, last, first)


def band(py):
    k = iota2((py, py), 0)
    j = iota2((py, py), 1)
    d = k - j
    one = jnp.where(d == 1, 8.0, jnp.where(d == -1, -8.0, 0.0))
    two = jnp.where(d == 2, -1.0, jnp.where(d == -2, 1.0, 0.0))
    return (one + two).astype(bf16)


def rim_band(py):
    k = iota2((4, py), 0)
    j = iota2((4, py), 1)
    d = jnp.where(k < 2, k - 2, py - 2 + k) - j
    one = jnp.where(d == 1, 8.0, jnp.where(d == -1, -8.0, 0.0))
    two = jnp.where(d == 2, -1.0, jnp.where(d == -2, 1.0, 0.0))
    return (one + two).astype(bf16)


def second_inner(field):
    center = band(field.shape[1])
    total = 0.0
    for piece in split(field):
        total = total + jnp.dot(piece, center, preferred_element_type=f32)
    return total * (1.0 / 12.0)


def second_rim(rim, py):
    edge = rim_band(py)
    total = 0.0
    for piece in split(rim):
        total = total + lax.dot_general(
            piece, edge, (((0,), (0,)), ((), ())), preferred_element_type=f32
        )
    return total * (1.0 / 12.0)


def first_inner(rows, i, px):
    one = rows(i + 1) if i + 1 < px else 0.0
    one = one - rows(i - 1) if i >= 1 else one
    two = rows(i + 2) if i + 2 < px else 0.0
    two = two - rows(i - 2) if i >= 2 else two
    return (8.0 * one - two) * (1.0 / 12.0)


def first_rim(i, before, after, px):
    if i == 0:
        return (before[0] - 8.0 * before[1]) * (1.0 / 12.0)
    if i == 1:
        return before[1] * (1.0 / 12.0)
    if i == px - 2:
        return after[0] * (-1.0 / 12.0)
    return (8.0 * after[0] - after[1]) * (1.0 / 12.0)


def first_inner(rows, i, px):
    one = rows(i + 1) if i + 1 < px else 0.0
    one = one - rows(i - 1) if i >= 1 else one
    two = rows(i + 2) if i + 2 < px else 0.0
    two = two - rows(i - 2) if i >= 2 else two
    return (8.0 * one - two) * (1.0 / 12.0)


def first_rim(i, before, after, px):
    if i == 0:
        return (before[0] - 8.0 * before[1]) * (1.0 / 12.0)
    if i == 1:
        return before[1] * (1.0 / 12.0)
    if i == px - 2:
        return after[0] * (-1.0 / 12.0)
    return (8.0 * after[0] - after[1]) * (1.0 / 12.0)


def winds_inner(px, u_ref, v_ref, p_ref, g_ref, q_ref, uo_ref, vo_ref, po_ref, pr_ref, gv_ref):
    levels = u_ref.shape[0] // px
    pressure = p_ref[...] * q_ref[...]
    pr_ref[...] = pressure
    vo_ref[...] = v_ref[...] + second_inner(pressure)
    gv_ref[...] = second_inner(v_ref[...])

    def u_rows(i):
        return row(u_ref, i, levels, px)

    def p_rows(i):
        return row(pr_ref, i, levels, px)

    for i in range(px):
        here = pl.ds(i, levels, stride=px)
        uo_ref[here, :] = u_ref[here, :] + first_inner(p_rows, i, px)
        po_ref[here, :] = p_ref[here, :] + g_ref[here, :] * (
            first_inner(u_rows, i, px) + gv_ref[here, :]
        )


def theta_inner(px, rim_ref, inner_ref, mt_ref, wf_ref, ws_ref, o_ref, star_ref, first_ref):
    levels = inner_ref.shape[1]
    for i in range(px):
        if 2 <= i < px - 2:
            got = inner_ref[i - 2]
        else:
            got = rim_ref[pl.ds(rim_slot(i, px) * levels, levels), :]
        star = got + row(mt_ref, i, levels, px)
        star_ref[pl.ds(i, levels, stride=px), :] = star
        first_ref[i] = row(wf_ref, i, levels, px) * star
    star = star_ref[...]
    star_ref[...] = star + second_inner(ws_ref[...] * star)

    def rows(i):
        return first_ref[i]

    for i in range(px):
        here = pl.ds(i, levels, stride=px)
        o_ref[here, :] = star_ref[here, :] + first_inner(rows, i, px)


def halo_rows(e4_ref, o4_ref, at, odd):
    before = [jnp.where(odd, e4_ref[at, d], o4_ref[at, d]) for d in range(2)]
    after = [jnp.where(odd, o4_ref[at, d], e4_ref[at, d]) for d in range(2)]
    return before, after


def halo_columns(e1_ref, o1_ref, at, odd):
    e1 = e1_ref[2 * at : 2 * at + 2]
    o1 = o1_ref[2 * at : 2 * at + 2]
    return jnp.concatenate([jnp.where(odd, e1, o1), jnp.where(odd, o1, e1)], axis=0)


def parities():
    cols = lax.axis_index("cols")
    return lax.rem(lax.div(cols, TW), 2) == 1, lax.rem(cols, 2) == 1


def finish(px, ub_ref, vb_ref, pb_ref, g_ref, tb_ref, e4_ref, o4_ref, e1_ref, o1_ref,
           u_hbm, v_hbm, t_hbm, p_hbm, u_ref, v_ref, t_ref, p_ref, sems):
    cells, py = ub_ref.shape
    levels = cells // px
    odd4, odd1 = parities()
    copies, send = sender(sems)
    edge_rows = (0, 1, px - 2, px - 1)
    u_ref[...] = ub_ref[...]
    before, after = halo_rows(e4_ref, o4_ref, 1, odd4)
    for i in edge_rows:
        here = pl.ds(i, levels, stride=px)
        u_ref[here, :] = ub_ref[here, :] + first_rim(i, before, after, px)
    send(u_ref, u_hbm)
    v_ref[...] = vb_ref[...] + second_rim(halo_columns(e1_ref, o1_ref, 1, odd1), py)
    send(v_ref, v_hbm)
    t_ref[...] = tb_ref[...] + second_rim(halo_columns(e1_ref, o1_ref, 2, odd1), py)
    before, after = halo_rows(e4_ref, o4_ref, 2, odd4)
    for i in edge_rows:
        here = pl.ds(i, levels, stride=px)
        t_ref[here, :] = t_ref[here, :] + first_rim(i, before, after, px)
    send(t_ref, t_hbm)
    p_ref[...] = pb_ref[...] + g_ref[...] * second_rim(halo_columns(e1_ref, o1_ref, 0, odd1), py)
    before, after = halo_rows(e4_ref, o4_ref, 0, odd4)
    for i in edge_rows:
        here = pl.ds(i, levels, stride=px)
        p_ref[here, :] = p_ref[here, :] + g_ref[here, :] * first_rim(i, before, after, px)
    send(p_ref, p_hbm)
    for copy in copies:
        copy.wait()


def kernel_for(px, body):
    def kernel(*refs):
        body(px, *refs)

    return kernel


def exchange(array, step, odd_pairs):
    devices = lax.axis_size("cols")
    pairs = []
    for c in range(devices):
        up = ((c // step) % 2 == 1) == odd_pairs
        pairs.append((c, (c + step if up else c - step) % devices))
    return lax.ppermute(array, "cols", pairs)


def on_device(u, v, w, t, p, grad, squeeze, wind_first, wind_second, a):
    levels, _, px, py = u.shape
    cells = levels * px
    u2, v2, w2, t2, p2, g2, q2, wf2, ws2 = (
        x.reshape(cells, py) for x in (u, v, w, t, p, grad, squeeze, wind_first, wind_second)
    )
    at = pltpu.VMEM((4 * levels, 2 * levels), f32)
    flat = (cells, py)
    rim_rows = 4 * levels + 4 * (cells // py)
    rim_shape = (rim_rows, py)
    inner_shape = (px - 4, levels, py)
    (rim_t,) = call(
        kernel_for(px, solve_rim), "solve_rim", [rim_shape],
        [pltpu.VMEM(flat, f32), pltpu.VMEM(flat, f32), pltpu.VMEM(a.shape, f32), at,
         pltpu.VMEM(flat, f32), pltpu.SemaphoreType.DMA((3,))],
        w2, t2, a, in_space=HBM, limit=FIRST_LIMIT, flops=LONG)
    inner_t, mine_t = call(
        kernel_for(px, solve_inner), "solve_inner", [inner_shape, flat], [at], w2, t2, a,
        after=(rim_t,), flops=I_COST)
    got_rim = passed_along(rim_t, "lev", 1)
    got_inner = passed_along(inner_t, "lev", 1)
    other_w, mine_w = call(
        kernel_for(px, solve_w), "solve_w", [flat] * 2, [at], w2, t2, a, flops=LONG, after=(inner_t,))
    o4, e1, o1 = call(
        kernel_for(px, pack), "pack", [(3, 2, levels, py)] + [(8, cells)] * 2, [],
        u2, v2, p2, q2, wf2, ws2, mine_t, got_rim, flops=LONG, after=(other_w,))
    (e4,) = call(
        kernel_for(px, pack_even), "pack_even", [(3, 2, levels, py)], [],
        u2, p2, q2, wf2, mine_t, got_rim, flops=LONG, after=(o1,))
    got_w = passed_along(other_w, "lev", 1)
    halos = (exchange(e4, TW, False), exchange(o4, TW, True), exchange(e1, 1, False), exchange(o1, 1, True))
    u_in, v_in, p_in = call(
        kernel_for(px, winds_inner), "winds_inner", [flat] * 3, [pltpu.VMEM(flat, f32)] * 2,
        u2, v2, p2, g2, q2, after=(e4,), flops=W_COST)
    (t_in,) = call(
        kernel_for(px, theta_inner), "theta_inner", [flat],
        [pltpu.VMEM(flat, f32), pltpu.VMEM((px, levels, py), f32)],
        got_rim, got_inner, mine_t, wf2, ws2, flops=T_COST)
    w_out = mine_w + got_w
    u_out, v_out, theta_out, p_out = call(
        kernel_for(px, finish), "finish", [flat] * 4,
        [pltpu.VMEM(flat, f32)] * 4 + [pltpu.SemaphoreType.DMA((4,))],
        u_in, v_in, p_in, g2, t_in, *halos, out_space=HBM, flops=F_COST)
    outs = (u_out, v_out, w_out, theta_out, p_out)
    return tuple(x.reshape(u.shape) for x in outs)


def solution(mesh):
    spread = P("lev", "cols", None, None)
    return jax.shard_map(
        on_device,
        mesh=mesh,
        in_specs=(spread,) * 9 + (P(),),
        out_specs=(spread,) * 5,
        check_vma=False,
    )
```

```python
import jax
import jax.numpy as jnp
from jax import lax
from jax.experimental import pallas as pl
from jax.experimental.pallas import tpu as pltpu
from jax.sharding import PartitionSpec as P

TW = 4
FIRST_LIMIT = (53 << 20) + (640 << 10)
LONG = 12_000_000_000
W_COST = 0
I_COST = 0
T_COST = 0
F_COST = 0
f32 = jnp.float32
bf16 = jnp.bfloat16
VMEM = pl.BlockSpec(memory_space=pltpu.VMEM)


def passed_along(array, axis, by):
    devices = lax.axis_size(axis)
    return lax.ppermute(array, axis, [(i, (i + by) % devices) for i in range(devices)])


def split(x):
    high = x.astype(bf16)
    return high, (x - high.astype(f32)).astype(bf16)


def split3(x):
    high = x.astype(bf16)
    rest = x - high.astype(f32)
    middle = rest.astype(bf16)
    return high, middle, (rest - middle.astype(f32)).astype(bf16)


HBM = pl.BlockSpec(memory_space=pl.ANY)


def call(kernel, name, outs, scratch, *args, flops=0, in_space=VMEM, out_space=VMEM, limit=32 << 20, after=()):
    shapes = tuple(jax.ShapeDtypeStruct(s, f32) for s in outs)
    size = sum(a.size for a in args) + sum(s.size for s in shapes)

    def body(*refs):
        kernel(*refs[: len(args)], *refs[len(args) + len(after) :])

    return pl.pallas_call(
        body,
        out_shape=shapes,
        in_specs=[in_space] * len(args) + [HBM] * len(after),
        out_specs=out_space if isinstance(out_space, tuple) else (out_space,) * len(shapes),
        scratch_shapes=scratch,
        name=name,
        cost_estimate=pl.CostEstimate(flops=flops, bytes_accessed=4 * size, transcendentals=0),
        compiler_params=pltpu.CompilerParams(vmem_limit_bytes=limit),
    )(*args, *after)


def row(ref, i, levels, px):
    return ref[pl.ds(i, levels, stride=px), :]


def left_factor(blocks):
    high, low = split(jnp.concatenate(blocks, axis=0))
    return jnp.concatenate(
        [jnp.concatenate([high, high], axis=1), jnp.concatenate([low, low], axis=1)], axis=0
    )


def paired(pieces):
    halves = []
    for w_part, t_part in pieces:
        halves.append(jnp.concatenate(split(jnp.concatenate([w_part, t_part], axis=0)), axis=0))
    return jnp.concatenate(halves, axis=1)


def iota2(shape, dim):
    return lax.broadcasted_iota(jnp.int32, shape, dim)


def rim_selector(py):
    k = iota2((8, py), 0)
    j = iota2((8, py), 1)
    want = jnp.where(k < 2, k, py - 4 + k)
    return jnp.where((j == want) & (k < 4), 1.0, 0.0).astype(bf16)


def rims(field, selector):
    total = 0.0
    for piece in split3(field):
        total = total + lax.dot_general(
            selector, piece, (((1,), (1,)), ((), ())), preferred_element_type=f32
        )
    return total


def rim_slot(i, px):
    return i if i < 2 else i - px + 4


def sender(sems):
    copies = []

    def send(source, target):
        copy = pltpu.make_async_copy(source, target, sems.at[len(copies)])
        copy.start()
        copies.append(copy)

    return copies, send


def solve_first(px, w_hbm, t_hbm, a_hbm, rim_ref, at_ref, w_ref, t_ref, a_ref, full_ref, sems):
    cells, py = w_hbm.shape
    levels = cells // px
    copies, send = sender(sems)
    send(a_hbm, a_ref)
    send(w_hbm, w_ref)
    send(t_hbm, t_ref)
    me = lax.axis_index("lev")
    copies[0].wait()
    rows = jnp.concatenate(
        [a_ref[pl.ds(me * levels, levels), :], a_ref[pl.ds((2 + me) * levels, levels), :]], axis=0
    )
    at_ref[...] = rows.T
    left = left_factor([at_ref[pl.ds((3 - me) * levels, levels), :]])
    copies[1].wait()
    copies[2].wait()
    for i, part in solved(px, left, w_ref, t_ref):
        full_ref[pl.ds(i, levels, stride=px), :] = part
        if not 2 <= i < px - 2:
            rim_ref[pl.ds(rim_slot(i, px) * levels, levels), :] = part
    edges = rims(full_ref[...], rim_selector(py))
    for k in range(levels * px // py):
        rim_ref[pl.ds(4 * levels + 4 * k, 4), :] = edges[0:4, k * py : (k + 1) * py]


def solved(px, left, w_ref, t_ref, skip=0):
    levels = w_ref.shape[0] // px
    py = w_ref.shape[1]
    half = left.shape[0] // 2
    for i in range(skip, px - skip, 2):
        right = paired([(row(w_ref, i + d, levels, px), row(t_ref, i + d, levels, px)) for d in range(2)])
        r = jnp.dot(left, right, preferred_element_type=f32)
        r = r[:half] + r[half:]
        yield i, r[:, :py]
        yield i + 1, r[:, py:]


def solve_inner(px, w_ref, t_ref, at_ref, inner_ref):
    levels = w_ref.shape[0] // px
    me = lax.axis_index("lev")
    left = left_factor([at_ref[pl.ds((3 - me) * levels, levels), :]])
    for i, part in solved(px, left, w_ref, t_ref, 2):
        inner_ref[i - 2] = part


def solve_rest(px, w_ref, t_ref, at_ref, ow_ref, mw_ref, mt_ref):
    levels = w_ref.shape[0] // px
    me = lax.axis_index("lev")
    left = left_factor(
        [
            at_ref[pl.ds((1 - me) * levels, levels), :],
            at_ref[pl.ds(me * levels, levels), :],
            at_ref[pl.ds((2 + me) * levels, levels), :],
        ]
    )
    for i, part in solved(px, left, w_ref, t_ref):
        here = pl.ds(i, levels, stride=px)
        ow_ref[here, :] = part[:levels]
        mw_ref[here, :] = part[levels : 2 * levels]
        mt_ref[here, :] = part[2 * levels :]


def pack_rows(px, first, u_ref, p_ref, q_ref, wf_ref, mt_ref, got_ref, out):
    levels = out.shape[2]
    start = (1 - first) * (px - 2)
    for d in range(2):
        i = start + d
        out[0, d] = row(u_ref, i, levels, px)
        out[1, d] = row(p_ref, i, levels, px) * row(q_ref, i, levels, px)
        star = row(mt_ref, i, levels, px) + got_ref[pl.ds(((1 - first) * 2 + d) * levels, levels), :]
        out[2, d] = row(wf_ref, i, levels, px) * star


def pack_even(px, u_ref, p_ref, q_ref, wf_ref, mt_ref, got_ref, e4_ref):
    odd4 = lax.rem(lax.div(lax.axis_index("cols"), TW), 2)
    pack_rows(px, odd4, u_ref, p_ref, q_ref, wf_ref, mt_ref, got_ref, e4_ref)


def pack(px, u_ref, v_ref, p_ref, q_ref, wf_ref, ws_ref, mt_ref, got_ref, o4_ref, e1_ref, o1_ref):
    levels = o4_ref.shape[2]
    py = o4_ref.shape[3]
    cols = lax.axis_index("cols")
    odd4 = lax.rem(lax.div(cols, TW), 2)
    odd1 = lax.rem(cols, 2)
    pack_rows(px, 1 - odd4, u_ref, p_ref, q_ref, wf_ref, mt_ref, got_ref, o4_ref)
    selector = rim_selector(py)
    got_rims = jnp.concatenate(
        [got_ref[pl.ds(4 * levels + 4 * k, 4), :] for k in range(levels * px // py)], axis=1
    )
    v_rims = rims(v_ref[...], selector)[0:4]
    p_rims = rims(p_ref[...] * q_ref[...], selector)[0:4]
    t_rims = rims(ws_ref[...], selector)[0:4] * (rims(mt_ref[...], selector)[0:4] + got_rims)
    first = jnp.concatenate([v_rims[0:2], p_rims[0:2], t_rims[0:2], t_rims[0:2]], axis=0)
    last = jnp.concatenate([v_rims[2:4], p_rims[2:4], t_rims[2:4], t_rims[2:4]], axis=0)
    is_odd = odd1 == 1
    e1_ref[...] = jnp.where(is_odd, first, last)
    o1_ref[...] = jnp.where(is_odd, last, first)


def band(py):
    k = iota2((py, py), 0)
    j = iota2((py, py), 1)
    d = k - j
    one = jnp.where(d == 1, 8.0, jnp.where(d == -1, -8.0, 0.0))
    two = jnp.where(d == 2, -1.0, jnp.where(d == -2, 1.0, 0.0))
    return (one + two).astype(bf16)


def rim_band(py):
    k = iota2((4, py), 0)
    j = iota2((4, py), 1)
    d = jnp.where(k < 2, k - 2, py - 2 + k) - j
    one = jnp.where(d == 1, 8.0, jnp.where(d == -1, -8.0, 0.0))
    two = jnp.where(d == 2, -1.0, jnp.where(d == -2, 1.0, 0.0))
    return (one + two).astype(bf16)


def second_inner(field):
    center = band(field.shape[1])
    total = 0.0
    for piece in split(field):
        total = total + jnp.dot(piece, center, preferred_element_type=f32)
    return total * (1.0 / 12.0)


def second_rim(rim, py):
    edge = rim_band(py)
    total = 0.0
    for piece in split(rim):
        total = total + lax.dot_general(
            piece, edge, (((0,), (0,)), ((), ())), preferred_element_type=f32
        )
    return total * (1.0 / 12.0)


def first_inner(rows, i, px):
    one = rows(i + 1) if i + 1 < px else 0.0
    one = one - rows(i - 1) if i >= 1 else one
    two = rows(i + 2) if i + 2 < px else 0.0
    two = two - rows(i - 2) if i >= 2 else two
    return (8.0 * one - two) * (1.0 / 12.0)


def first_rim(i, before, after, px):
    if i == 0:
        return (before[0] - 8.0 * before[1]) * (1.0 / 12.0)
    if i == 1:
        return before[1] * (1.0 / 12.0)
    if i == px - 2:
        return after[0] * (-1.0 / 12.0)
    return (8.0 * after[0] - after[1]) * (1.0 / 12.0)


def first_inner(rows, i, px):
    one = rows(i + 1) if i + 1 < px else 0.0
    one = one - rows(i - 1) if i >= 1 else one
    two = rows(i + 2) if i + 2 < px else 0.0
    two = two - rows(i - 2) if i >= 2 else two
    return (8.0 * one - two) * (1.0 / 12.0)


def first_rim(i, before, after, px):
    if i == 0:
        return (before[0] - 8.0 * before[1]) * (1.0 / 12.0)
    if i == 1:
        return before[1] * (1.0 / 12.0)
    if i == px - 2:
        return after[0] * (-1.0 / 12.0)
    return (8.0 * after[0] - after[1]) * (1.0 / 12.0)


def winds_inner(px, u_ref, v_ref, p_ref, g_ref, q_ref, uo_ref, vo_ref, po_ref, pr_ref, gv_ref):
    levels = u_ref.shape[0] // px
    pressure = p_ref[...] * q_ref[...]
    pr_ref[...] = pressure
    vo_ref[...] = v_ref[...] + second_inner(pressure)
    gv_ref[...] = second_inner(v_ref[...])

    def u_rows(i):
        return row(u_ref, i, levels, px)

    def p_rows(i):
        return row(pr_ref, i, levels, px)

    for i in range(px):
        here = pl.ds(i, levels, stride=px)
        uo_ref[here, :] = u_ref[here, :] + first_inner(p_rows, i, px)
        po_ref[here, :] = p_ref[here, :] + g_ref[here, :] * (
            first_inner(u_rows, i, px) + gv_ref[here, :]
        )


def theta_inner(px, rim_ref, inner_ref, mt_ref, wf_ref, ws_ref, o_ref, star_ref, first_ref):
    levels = inner_ref.shape[1]
    for i in range(px):
        if 2 <= i < px - 2:
            got = inner_ref[i - 2]
        else:
            got = rim_ref[pl.ds(rim_slot(i, px) * levels, levels), :]
        star = got + row(mt_ref, i, levels, px)
        star_ref[pl.ds(i, levels, stride=px), :] = star
        first_ref[i] = row(wf_ref, i, levels, px) * star
    star = star_ref[...]
    star_ref[...] = star + second_inner(ws_ref[...] * star)

    def rows(i):
        return first_ref[i]

    for i in range(px):
        here = pl.ds(i, levels, stride=px)
        o_ref[here, :] = star_ref[here, :] + first_inner(rows, i, px)


def halo_rows(e4_ref, o4_ref, at, odd):
    before = [jnp.where(odd, e4_ref[at, d], o4_ref[at, d]) for d in range(2)]
    after = [jnp.where(odd, o4_ref[at, d], e4_ref[at, d]) for d in range(2)]
    return before, after


def halo_columns(e1_ref, o1_ref, at, odd):
    e1 = e1_ref[2 * at : 2 * at + 2]
    o1 = o1_ref[2 * at : 2 * at + 2]
    return jnp.concatenate([jnp.where(odd, e1, o1), jnp.where(odd, o1, e1)], axis=0)


def parities():
    cols = lax.axis_index("cols")
    return lax.rem(lax.div(cols, TW), 2) == 1, lax.rem(cols, 2) == 1


def finish(px, ub_ref, vb_ref, pb_ref, g_ref, tb_ref, e4_ref, o4_ref, e1_ref, o1_ref,
           u_hbm, v_hbm, t_hbm, p_hbm, u_ref, v_ref, t_ref, p_ref, sems):
    cells, py = ub_ref.shape
    levels = cells // px
    odd4, odd1 = parities()
    copies, send = sender(sems)
    edge_rows = (0, 1, px - 2, px - 1)
    u_ref[...] = ub_ref[...]
    before, after = halo_rows(e4_ref, o4_ref, 1, odd4)
    for i in edge_rows:
        here = pl.ds(i, levels, stride=px)
        u_ref[here, :] = ub_ref[here, :] + first_rim(i, before, after, px)
    send(u_ref, u_hbm)
    v_ref[...] = vb_ref[...] + second_rim(halo_columns(e1_ref, o1_ref, 1, odd1), py)
    send(v_ref, v_hbm)
    t_ref[...] = tb_ref[...] + second_rim(halo_columns(e1_ref, o1_ref, 2, odd1), py)
    before, after = halo_rows(e4_ref, o4_ref, 2, odd4)
    for i in edge_rows:
        here = pl.ds(i, levels, stride=px)
        t_ref[here, :] = t_ref[here, :] + first_rim(i, before, after, px)
    send(t_ref, t_hbm)
    p_ref[...] = pb_ref[...] + g_ref[...] * second_rim(halo_columns(e1_ref, o1_ref, 0, odd1), py)
    before, after = halo_rows(e4_ref, o4_ref, 0, odd4)
    for i in edge_rows:
        here = pl.ds(i, levels, stride=px)
        p_ref[here, :] = p_ref[here, :] + g_ref[here, :] * first_rim(i, before, after, px)
    send(p_ref, p_hbm)
    for copy in copies:
        copy.wait()


def kernel_for(px, body):
    def kernel(*refs):
        body(px, *refs)

    return kernel


def exchange(array, step, odd_pairs):
    devices = lax.axis_size("cols")
    pairs = []
    for c in range(devices):
        up = ((c // step) % 2 == 1) == odd_pairs
        pairs.append((c, (c + step if up else c - step) % devices))
    return lax.ppermute(array, "cols", pairs)


def on_device(u, v, w, t, p, grad, squeeze, wind_first, wind_second, a):
    levels, _, px, py = u.shape
    cells = levels * px
    u2, v2, w2, t2, p2, g2, q2, wf2, ws2 = (
        x.reshape(cells, py) for x in (u, v, w, t, p, grad, squeeze, wind_first, wind_second)
    )
    flat = (cells, py)
    rim_rows = 4 * levels + 4 * (cells // py)
    rim_shape = (rim_rows, py)
    inner_shape = (px - 4, levels, py)
    rim_t, at = call(
        kernel_for(px, solve_first), "solve_first", [rim_shape, (4 * levels, 2 * levels)],
        [pltpu.VMEM(flat, f32), pltpu.VMEM(flat, f32), pltpu.VMEM(a.shape, f32),
         pltpu.VMEM(flat, f32), pltpu.SemaphoreType.DMA((3,))],
        w2, t2, a, in_space=HBM, limit=FIRST_LIMIT, flops=LONG)
    (inner_t,) = call(
        kernel_for(px, solve_inner), "solve_inner", [inner_shape], [], w2, t2, at, flops=I_COST)
    got_rim = passed_along(rim_t, "lev", 1)
    got_inner = passed_along(inner_t, "lev", 1)
    other_w, mine_w, mine_t = call(
        kernel_for(px, solve_rest), "solve_rest", [flat] * 3, [], w2, t2, at, flops=LONG, after=(inner_t,))
    o4, e1, o1 = call(
        kernel_for(px, pack), "pack", [(3, 2, levels, py)] + [(8, cells)] * 2, [],
        u2, v2, p2, q2, wf2, ws2, mine_t, got_rim, flops=LONG, after=(other_w,))
    (e4,) = call(
        kernel_for(px, pack_even), "pack_even", [(3, 2, levels, py)], [],
        u2, p2, q2, wf2, mine_t, got_rim, flops=LONG, after=(o1,))
    got_w = passed_along(other_w, "lev", 1)
    halos = (exchange(e4, TW, False), exchange(o4, TW, True), exchange(e1, 1, False), exchange(o1, 1, True))
    u_in, v_in, p_in = call(
        kernel_for(px, winds_inner), "winds_inner", [flat] * 3, [pltpu.VMEM(flat, f32)] * 2,
        u2, v2, p2, g2, q2, after=(e4,), flops=W_COST)
    (t_in,) = call(
        kernel_for(px, theta_inner), "theta_inner", [flat],
        [pltpu.VMEM(flat, f32), pltpu.VMEM((px, levels, py), f32)],
        got_rim, got_inner, mine_t, wf2, ws2, flops=T_COST)
    w_out = mine_w + got_w
    u_out, v_out, theta_out, p_out = call(
        kernel_for(px, finish), "finish", [flat] * 4,
        [pltpu.VMEM(flat, f32)] * 4 + [pltpu.SemaphoreType.DMA((4,))],
        u_in, v_in, p_in, g2, t_in, *halos, out_space=HBM, flops=F_COST)
    outs = (u_out, v_out, w_out, theta_out, p_out)
    return tuple(x.reshape(u.shape) for x in outs)


def solution(mesh):
    spread = P("lev", "cols", None, None)
    return jax.shard_map(
        on_device,
        mesh=mesh,
        in_specs=(spread,) * 9 + (P(),),
        out_specs=(spread,) * 5,
        check_vma=False,
    )
```

```python
import jax
import jax.numpy as jnp
from jax import lax
from jax.experimental import pallas as pl
from jax.experimental.pallas import tpu as pltpu
from jax.sharding import PartitionSpec as P

TW = 4
FIRST_LIMIT = (53 << 20) + (640 << 10)
LONG = 12_000_000_000
W_COST = 0
I_COST = 0
T_COST = 0
F_COST = 0
f32 = jnp.float32
bf16 = jnp.bfloat16
VMEM = pl.BlockSpec(memory_space=pltpu.VMEM)


def passed_along(array, axis, by):
    devices = lax.axis_size(axis)
    return lax.ppermute(array, axis, [(i, (i + by) % devices) for i in range(devices)])


def split(x):
    high = x.astype(bf16)
    return high, (x - high.astype(f32)).astype(bf16)


def split3(x):
    high = x.astype(bf16)
    rest = x - high.astype(f32)
    middle = rest.astype(bf16)
    return high, middle, (rest - middle.astype(f32)).astype(bf16)


HBM = pl.BlockSpec(memory_space=pl.ANY)


def call(kernel, name, outs, scratch, *args, flops=0, in_space=VMEM, out_space=VMEM, limit=32 << 20, after=()):
    shapes = tuple(jax.ShapeDtypeStruct(s, f32) for s in outs)
    size = sum(a.size for a in args) + sum(s.size for s in shapes)

    def body(*refs):
        kernel(*refs[: len(args)], *refs[len(args) + len(after) :])

    return pl.pallas_call(
        body,
        out_shape=shapes,
        in_specs=[in_space] * len(args) + [HBM] * len(after),
        out_specs=out_space if isinstance(out_space, tuple) else (out_space,) * len(shapes),
        scratch_shapes=scratch,
        name=name,
        cost_estimate=pl.CostEstimate(flops=flops, bytes_accessed=4 * size, transcendentals=0),
        compiler_params=pltpu.CompilerParams(vmem_limit_bytes=limit),
    )(*args, *after)


def row(ref, i, levels, px):
    return ref[pl.ds(i, levels, stride=px), :]


def left_factor(blocks):
    high, low = split(jnp.concatenate(blocks, axis=0))
    return jnp.concatenate(
        [jnp.concatenate([high, high], axis=1), jnp.concatenate([low, low], axis=1)], axis=0
    )


def paired(pieces):
    halves = []
    for w_part, t_part in pieces:
        halves.append(jnp.concatenate(split(jnp.concatenate([w_part, t_part], axis=0)), axis=0))
    return jnp.concatenate(halves, axis=1)


def iota2(shape, dim):
    return lax.broadcasted_iota(jnp.int32, shape, dim)


def rim_selector(py):
    k = iota2((8, py), 0)
    j = iota2((8, py), 1)
    want = jnp.where(k < 2, k, py - 4 + k)
    return jnp.where((j == want) & (k < 4), 1.0, 0.0).astype(bf16)


def rims(field, selector):
    total = 0.0
    for piece in split3(field):
        total = total + lax.dot_general(
            selector, piece, (((1,), (1,)), ((), ())), preferred_element_type=f32
        )
    return total


def rim_slot(i, px):
    return i if i < 2 else i - px + 4


def sender(sems):
    copies = []

    def send(source, target):
        copy = pltpu.make_async_copy(source, target, sems.at[len(copies)])
        copy.start()
        copies.append(copy)

    return copies, send


def solve_first(px, w_hbm, t_hbm, a_hbm, rim_ref, at_ref, w_ref, t_ref, a_ref, full_ref, sems):
    levels, _, py = w_hbm.shape
    half = px // 2
    copies, send = sender(sems)
    send(a_hbm, a_ref)
    for h in range(2):
        here = pl.ds(h * half, half)
        send(w_hbm.at[:, here, :], w_ref.at[h])
        send(t_hbm.at[:, here, :], t_ref.at[h])
    me = lax.axis_index("lev")
    copies[0].wait()
    rows = jnp.concatenate(
        [a_ref[pl.ds(me * levels, levels), :], a_ref[pl.ds((2 + me) * levels, levels), :]], axis=0
    )
    at_ref[...] = rows.T
    left = left_factor([at_ref[pl.ds((3 - me) * levels, levels), :]])
    for h in range(2):
        copies[1 + 2 * h].wait()
        copies[2 + 2 * h].wait()
        w_half = w_ref.at[h].reshape(levels * half, py)
        t_half = t_ref.at[h].reshape(levels * half, py)
        for k, part in solved(half, left, w_half, t_half):
            i = h * half + k
            full_ref[pl.ds(i, levels, stride=px), :] = part
            if not 2 <= i < px - 2:
                rim_ref[pl.ds(rim_slot(i, px) * levels, levels), :] = part
    edges = rims(full_ref[...], rim_selector(py))
    for k in range(levels * px // py):
        rim_ref[pl.ds(4 * levels + 4 * k, 4), :] = edges[0:4, k * py : (k + 1) * py]


def solved(px, left, w_ref, t_ref, skip=0):
    levels = w_ref.shape[0] // px
    py = w_ref.shape[1]
    half = left.shape[0] // 2
    for i in range(skip, px - skip, 2):
        right = paired([(row(w_ref, i + d, levels, px), row(t_ref, i + d, levels, px)) for d in range(2)])
        r = jnp.dot(left, right, preferred_element_type=f32)
        r = r[:half] + r[half:]
        yield i, r[:, :py]
        yield i + 1, r[:, py:]


def solve_inner(px, w_ref, t_ref, at_ref, inner_ref):
    levels = w_ref.shape[0] // px
    me = lax.axis_index("lev")
    left = left_factor([at_ref[pl.ds((3 - me) * levels, levels), :]])
    for i, part in solved(px, left, w_ref, t_ref, 2):
        inner_ref[i - 2] = part


def solve_rest(px, w_ref, t_ref, at_ref, ow_ref, mw_ref, mt_ref):
    levels = w_ref.shape[0] // px
    me = lax.axis_index("lev")
    left = left_factor(
        [
            at_ref[pl.ds((1 - me) * levels, levels), :],
            at_ref[pl.ds(me * levels, levels), :],
            at_ref[pl.ds((2 + me) * levels, levels), :],
        ]
    )
    for i, part in solved(px, left, w_ref, t_ref):
        here = pl.ds(i, levels, stride=px)
        ow_ref[here, :] = part[:levels]
        mw_ref[here, :] = part[levels : 2 * levels]
        mt_ref[here, :] = part[2 * levels :]


def pack_rows(px, first, u_ref, p_ref, q_ref, wf_ref, mt_ref, got_ref, out):
    levels = out.shape[2]
    start = (1 - first) * (px - 2)
    for d in range(2):
        i = start + d
        out[0, d] = row(u_ref, i, levels, px)
        out[1, d] = row(p_ref, i, levels, px) * row(q_ref, i, levels, px)
        star = row(mt_ref, i, levels, px) + got_ref[pl.ds(((1 - first) * 2 + d) * levels, levels), :]
        out[2, d] = row(wf_ref, i, levels, px) * star


def pack_even(px, u_ref, p_ref, q_ref, wf_ref, mt_ref, got_ref, e4_ref):
    odd4 = lax.rem(lax.div(lax.axis_index("cols"), TW), 2)
    pack_rows(px, odd4, u_ref, p_ref, q_ref, wf_ref, mt_ref, got_ref, e4_ref)


def pack(px, u_ref, v_ref, p_ref, q_ref, wf_ref, ws_ref, mt_ref, got_ref, o4_ref, e1_ref, o1_ref):
    levels = o4_ref.shape[2]
    py = o4_ref.shape[3]
    cols = lax.axis_index("cols")
    odd4 = lax.rem(lax.div(cols, TW), 2)
    odd1 = lax.rem(cols, 2)
    pack_rows(px, 1 - odd4, u_ref, p_ref, q_ref, wf_ref, mt_ref, got_ref, o4_ref)
    selector = rim_selector(py)
    got_rims = jnp.concatenate(
        [got_ref[pl.ds(4 * levels + 4 * k, 4), :] for k in range(levels * px // py)], axis=1
    )
    v_rims = rims(v_ref[...], selector)[0:4]
    p_rims = rims(p_ref[...] * q_ref[...], selector)[0:4]
    t_rims = rims(ws_ref[...], selector)[0:4] * (rims(mt_ref[...], selector)[0:4] + got_rims)
    first = jnp.concatenate([v_rims[0:2], p_rims[0:2], t_rims[0:2]], axis=1)
    last = jnp.concatenate([v_rims[2:4], p_rims[2:4], t_rims[2:4]], axis=1)
    is_odd = odd1 == 1
    e1_ref[...] = jnp.where(is_odd, first, last)
    o1_ref[...] = jnp.where(is_odd, last, first)


def band(py):
    k = iota2((py, py), 0)
    j = iota2((py, py), 1)
    d = k - j
    one = jnp.where(d == 1, 8.0, jnp.where(d == -1, -8.0, 0.0))
    two = jnp.where(d == 2, -1.0, jnp.where(d == -2, 1.0, 0.0))
    return (one + two).astype(bf16)


def rim_band(py):
    k = iota2((4, py), 0)
    j = iota2((4, py), 1)
    d = jnp.where(k < 2, k - 2, py - 2 + k) - j
    one = jnp.where(d == 1, 8.0, jnp.where(d == -1, -8.0, 0.0))
    two = jnp.where(d == 2, -1.0, jnp.where(d == -2, 1.0, 0.0))
    return (one + two).astype(bf16)


def second_inner(field):
    center = band(field.shape[1])
    total = 0.0
    for piece in split(field):
        total = total + jnp.dot(piece, center, preferred_element_type=f32)
    return total * (1.0 / 12.0)


def second_rim(rim, py):
    edge = rim_band(py)
    total = 0.0
    for piece in split(rim):
        total = total + lax.dot_general(
            piece, edge, (((0,), (0,)), ((), ())), preferred_element_type=f32
        )
    return total * (1.0 / 12.0)


def first_inner(rows, i, px):
    one = rows(i + 1) if i + 1 < px else 0.0
    one = one - rows(i - 1) if i >= 1 else one
    two = rows(i + 2) if i + 2 < px else 0.0
    two = two - rows(i - 2) if i >= 2 else two
    return (8.0 * one - two) * (1.0 / 12.0)


def first_rim(i, before, after, px):
    if i == 0:
        return (before[0] - 8.0 * before[1]) * (1.0 / 12.0)
    if i == 1:
        return before[1] * (1.0 / 12.0)
    if i == px - 2:
        return after[0] * (-1.0 / 12.0)
    return (8.0 * after[0] - after[1]) * (1.0 / 12.0)


def first_inner(rows, i, px):
    one = rows(i + 1) if i + 1 < px else 0.0
    one = one - rows(i - 1) if i >= 1 else one
    two = rows(i + 2) if i + 2 < px else 0.0
    two = two - rows(i - 2) if i >= 2 else two
    return (8.0 * one - two) * (1.0 / 12.0)


def first_rim(i, before, after, px):
    if i == 0:
        return (before[0] - 8.0 * before[1]) * (1.0 / 12.0)
    if i == 1:
        return before[1] * (1.0 / 12.0)
    if i == px - 2:
        return after[0] * (-1.0 / 12.0)
    return (8.0 * after[0] - after[1]) * (1.0 / 12.0)


def winds_inner(px, u_ref, v_ref, p_ref, g_ref, q_ref, uo_ref, vo_ref, po_ref, pr_ref, gv_ref):
    levels = u_ref.shape[0] // px
    pressure = p_ref[...] * q_ref[...]
    pr_ref[...] = pressure
    vo_ref[...] = v_ref[...] + second_inner(pressure)
    gv_ref[...] = second_inner(v_ref[...])

    def u_rows(i):
        return row(u_ref, i, levels, px)

    def p_rows(i):
        return row(pr_ref, i, levels, px)

    for i in range(px):
        here = pl.ds(i, levels, stride=px)
        uo_ref[here, :] = u_ref[here, :] + first_inner(p_rows, i, px)
        po_ref[here, :] = p_ref[here, :] + g_ref[here, :] * (
            first_inner(u_rows, i, px) + gv_ref[here, :]
        )


def theta_inner(px, rim_ref, inner_ref, mt_ref, wf_ref, ws_ref, o_ref, star_ref, first_ref):
    levels = inner_ref.shape[1]
    for i in range(px):
        if 2 <= i < px - 2:
            got = inner_ref[i - 2]
        else:
            got = rim_ref[pl.ds(rim_slot(i, px) * levels, levels), :]
        star = got + row(mt_ref, i, levels, px)
        star_ref[pl.ds(i, levels, stride=px), :] = star
        first_ref[i] = row(wf_ref, i, levels, px) * star
    star = star_ref[...]
    star_ref[...] = star + second_inner(ws_ref[...] * star)

    def rows(i):
        return first_ref[i]

    for i in range(px):
        here = pl.ds(i, levels, stride=px)
        o_ref[here, :] = star_ref[here, :] + first_inner(rows, i, px)


def halo_rows(e4_ref, o4_ref, at, odd):
    before = [jnp.where(odd, e4_ref[at, d], o4_ref[at, d]) for d in range(2)]
    after = [jnp.where(odd, o4_ref[at, d], e4_ref[at, d]) for d in range(2)]
    return before, after


def halo_columns(e1_ref, o1_ref, at, odd):
    cells = e1_ref.shape[1] // 3
    e1 = e1_ref[:, at * cells : (at + 1) * cells]
    o1 = o1_ref[:, at * cells : (at + 1) * cells]
    return jnp.concatenate([jnp.where(odd, e1, o1), jnp.where(odd, o1, e1)], axis=0)


def parities():
    cols = lax.axis_index("cols")
    return lax.rem(lax.div(cols, TW), 2) == 1, lax.rem(cols, 2) == 1


def finish(px, ub_ref, vb_ref, pb_ref, g_ref, tb_ref, e4_ref, o4_ref, e1_ref, o1_ref,
           u_hbm, v_hbm, t_hbm, p_hbm, u_ref, v_ref, t_ref, p_ref, sems):
    cells, py = ub_ref.shape
    levels = cells // px
    odd4, odd1 = parities()
    copies, send = sender(sems)
    edge_rows = (0, 1, px - 2, px - 1)
    u_ref[...] = ub_ref[...]
    before, after = halo_rows(e4_ref, o4_ref, 1, odd4)
    for i in edge_rows:
        here = pl.ds(i, levels, stride=px)
        u_ref[here, :] = ub_ref[here, :] + first_rim(i, before, after, px)
    send(u_ref, u_hbm)
    v_ref[...] = vb_ref[...] + second_rim(halo_columns(e1_ref, o1_ref, 1, odd1), py)
    send(v_ref, v_hbm)
    t_ref[...] = tb_ref[...] + second_rim(halo_columns(e1_ref, o1_ref, 2, odd1), py)
    before, after = halo_rows(e4_ref, o4_ref, 2, odd4)
    for i in edge_rows:
        here = pl.ds(i, levels, stride=px)
        t_ref[here, :] = t_ref[here, :] + first_rim(i, before, after, px)
    send(t_ref, t_hbm)
    p_ref[...] = pb_ref[...] + g_ref[...] * second_rim(halo_columns(e1_ref, o1_ref, 0, odd1), py)
    before, after = halo_rows(e4_ref, o4_ref, 0, odd4)
    for i in edge_rows:
        here = pl.ds(i, levels, stride=px)
        p_ref[here, :] = p_ref[here, :] + g_ref[here, :] * first_rim(i, before, after, px)
    send(p_ref, p_hbm)
    for copy in copies:
        copy.wait()


def kernel_for(px, body):
    def kernel(*refs):
        body(px, *refs)

    return kernel


def exchange(array, step, odd_pairs):
    devices = lax.axis_size("cols")
    pairs = []
    for c in range(devices):
        up = ((c // step) % 2 == 1) == odd_pairs
        pairs.append((c, (c + step if up else c - step) % devices))
    return lax.ppermute(array, "cols", pairs)


def on_device(u, v, w, t, p, grad, squeeze, wind_first, wind_second, a):
    levels, _, px, py = u.shape
    cells = levels * px
    u2, v2, w2, t2, p2, g2, q2, wf2, ws2 = (
        x.reshape(cells, py) for x in (u, v, w, t, p, grad, squeeze, wind_first, wind_second)
    )
    flat = (cells, py)
    rim_rows = 4 * levels + 4 * (cells // py)
    rim_shape = (rim_rows, py)
    inner_shape = (px - 4, levels, py)
    rim_t, at = call(
        kernel_for(px, solve_first), "solve_first", [rim_shape, (4 * levels, 2 * levels)],
        [pltpu.VMEM((2, levels, px // 2, py), f32)] * 2
        + [pltpu.VMEM(a.shape, f32), pltpu.VMEM(flat, f32), pltpu.SemaphoreType.DMA((5,))],
        w.reshape(levels, px, py), t.reshape(levels, px, py), a, in_space=HBM, limit=FIRST_LIMIT, flops=LONG)
    (inner_t,) = call(
        kernel_for(px, solve_inner), "solve_inner", [inner_shape], [], w2, t2, at, flops=I_COST)
    got_rim = passed_along(rim_t, "lev", 1)
    got_inner = passed_along(inner_t, "lev", 1)
    other_w, mine_w, mine_t = call(
        kernel_for(px, solve_rest), "solve_rest", [flat] * 3, [], w2, t2, at, flops=LONG, after=(inner_t,))
    o4, e1, o1 = call(
        kernel_for(px, pack), "pack", [(3, 2, levels, py)] + [(2, 3 * cells)] * 2, [],
        u2, v2, p2, q2, wf2, ws2, mine_t, got_rim, flops=LONG, after=(other_w,))
    (e4,) = call(
        kernel_for(px, pack_even), "pack_even", [(3, 2, levels, py)], [],
        u2, p2, q2, wf2, mine_t, got_rim, flops=LONG, after=(o1,))
    got_w = passed_along(other_w, "lev", 1)
    halos = (exchange(e4, TW, False), exchange(o4, TW, True), exchange(e1, 1, False), exchange(o1, 1, True))
    u_in, v_in, p_in = call(
        kernel_for(px, winds_inner), "winds_inner", [flat] * 3, [pltpu.VMEM(flat, f32)] * 2,
        u2, v2, p2, g2, q2, after=(e4,), flops=W_COST)
    (t_in,) = call(
        kernel_for(px, theta_inner), "theta_inner", [flat],
        [pltpu.VMEM(flat, f32), pltpu.VMEM((px, levels, py), f32)],
        got_rim, got_inner, mine_t, wf2, ws2, flops=T_COST)
    w_out = mine_w + got_w
    u_out, v_out, theta_out, p_out = call(
        kernel_for(px, finish), "finish", [flat] * 4,
        [pltpu.VMEM(flat, f32)] * 4 + [pltpu.SemaphoreType.DMA((4,))],
        u_in, v_in, p_in, g2, t_in, *halos, out_space=HBM, flops=F_COST)
    outs = (u_out, v_out, w_out, theta_out, p_out)
    return tuple(x.reshape(u.shape) for x in outs)


def solution(mesh):
    spread = P("lev", "cols", None, None)
    return jax.shard_map(
        on_device,
        mesh=mesh,
        in_specs=(spread,) * 9 + (P(),),
        out_specs=(spread,) * 5,
        check_vma=False,
    )
```

```python
import jax
import jax.numpy as jnp
from jax import lax
from jax.experimental import pallas as pl
from jax.experimental.pallas import tpu as pltpu
from jax.sharding import PartitionSpec as P

TW = 4
EDGE = 3
FIRST_LIMIT = (53 << 20) + (560 << 10)
LONG = 12_000_000_000
W_COST = 0
I_COST = 0
T_COST = 0
F_COST = 0
f32 = jnp.float32
bf16 = jnp.bfloat16
VMEM = pl.BlockSpec(memory_space=pltpu.VMEM)


def passed_along(array, axis, by):
    devices = lax.axis_size(axis)
    return lax.ppermute(array, axis, [(i, (i + by) % devices) for i in range(devices)])


def split(x):
    high = x.astype(bf16)
    return high, (x - high.astype(f32)).astype(bf16)


def split3(x):
    high = x.astype(bf16)
    rest = x - high.astype(f32)
    middle = rest.astype(bf16)
    return high, middle, (rest - middle.astype(f32)).astype(bf16)


HBM = pl.BlockSpec(memory_space=pl.ANY)


def call(kernel, name, outs, scratch, *args, flops=0, in_space=VMEM, out_space=VMEM, limit=32 << 20, after=()):
    shapes = tuple(jax.ShapeDtypeStruct(s, f32) for s in outs)
    size = sum(a.size for a in args) + sum(s.size for s in shapes)

    def body(*refs):
        kernel(*refs[: len(args)], *refs[len(args) + len(after) :])

    return pl.pallas_call(
        body,
        out_shape=shapes,
        in_specs=[in_space] * len(args) + [HBM] * len(after),
        out_specs=out_space if isinstance(out_space, tuple) else (out_space,) * len(shapes),
        scratch_shapes=scratch,
        name=name,
        cost_estimate=pl.CostEstimate(flops=flops, bytes_accessed=4 * size, transcendentals=0),
        compiler_params=pltpu.CompilerParams(vmem_limit_bytes=limit),
    )(*args, *after)


def row(ref, i, levels, px):
    return ref[pl.ds(i, levels, stride=px), :]


def left_factor(blocks):
    high, low = split(jnp.concatenate(blocks, axis=0))
    return jnp.concatenate(
        [jnp.concatenate([high, high], axis=1), jnp.concatenate([low, low], axis=1)], axis=0
    )


def paired(pieces):
    halves = []
    for w_part, t_part in pieces:
        halves.append(jnp.concatenate(split(jnp.concatenate([w_part, t_part], axis=0)), axis=0))
    return jnp.concatenate(halves, axis=1)


def iota2(shape, dim):
    return lax.broadcasted_iota(jnp.int32, shape, dim)


def rim_selector(py):
    k = iota2((8, py), 0)
    j = iota2((8, py), 1)
    want = jnp.where(k < 2, k, py - 4 + k)
    return jnp.where((j == want) & (k < 4), 1.0, 0.0).astype(bf16)


def rims(field, selector):
    total = 0.0
    for piece in split3(field):
        total = total + lax.dot_general(
            selector, piece, (((1,), (1,)), ((), ())), preferred_element_type=f32
        )
    return total


def rim_slot(i, px):
    return i if i < EDGE else i - px + 2 * EDGE


def sender(sems):
    copies = []

    def send(source, target):
        copy = pltpu.make_async_copy(source, target, sems.at[len(copies)])
        copy.start()
        copies.append(copy)

    return copies, send


def solve_first(px, w_hbm, t_hbm, a_hbm, rim_ref, at_ref, w_ref, t_ref, a_ref, full_ref, sems):
    levels, _, py = w_hbm.shape
    half = px // 2
    copies, send = sender(sems)
    send(a_hbm, a_ref)
    for h in range(2):
        here = pl.ds(h * half, half)
        send(w_hbm.at[:, here, :], w_ref.at[h])
        send(t_hbm.at[:, here, :], t_ref.at[h])
    me = lax.axis_index("lev")
    copies[0].wait()
    rows = jnp.concatenate(
        [a_ref[pl.ds(me * levels, levels), :], a_ref[pl.ds((2 + me) * levels, levels), :]], axis=0
    )
    at_ref[...] = rows.T
    left = left_factor([at_ref[pl.ds((3 - me) * levels, levels), :]])
    for h in range(2):
        copies[1 + 2 * h].wait()
        copies[2 + 2 * h].wait()
        w_half = w_ref.at[h].reshape(levels * half, py)
        t_half = t_ref.at[h].reshape(levels * half, py)
        for k, part in solved(half, left, w_half, t_half):
            i = h * half + k
            full_ref[pl.ds(i, levels, stride=px), :] = part
            if not EDGE <= i < px - EDGE:
                rim_ref[pl.ds(rim_slot(i, px) * levels, levels), :] = part
    edges = rims(full_ref[...], rim_selector(py))
    for k in range(levels * px // py):
        rim_ref[pl.ds(2 * EDGE * levels + 4 * k, 4), :] = edges[0:4, k * py : (k + 1) * py]


def solved(px, left, w_ref, t_ref, skip=0):
    levels = w_ref.shape[0] // px
    py = w_ref.shape[1]
    half = left.shape[0] // 2
    for i in range(skip, px - skip, 2):
        right = paired([(row(w_ref, i + d, levels, px), row(t_ref, i + d, levels, px)) for d in range(2)])
        r = jnp.dot(left, right, preferred_element_type=f32)
        r = r[:half] + r[half:]
        yield i, r[:, :py]
        yield i + 1, r[:, py:]


def solve_inner(px, w_ref, t_ref, at_ref, inner_ref):
    levels = w_ref.shape[0] // px
    me = lax.axis_index("lev")
    left = left_factor([at_ref[pl.ds((3 - me) * levels, levels), :]])
    for i, part in solved(px, left, w_ref, t_ref, EDGE // 2 * 2):
        if EDGE <= i < px - EDGE:
            inner_ref[i - EDGE] = part


def solve_rest(px, w_ref, t_ref, at_ref, ow_ref, mw_ref, mt_ref):
    levels = w_ref.shape[0] // px
    me = lax.axis_index("lev")
    left = left_factor(
        [
            at_ref[pl.ds((1 - me) * levels, levels), :],
            at_ref[pl.ds(me * levels, levels), :],
            at_ref[pl.ds((2 + me) * levels, levels), :],
        ]
    )
    for i, part in solved(px, left, w_ref, t_ref):
        here = pl.ds(i, levels, stride=px)
        ow_ref[here, :] = part[:levels]
        mw_ref[here, :] = part[levels : 2 * levels]
        mt_ref[here, :] = part[2 * levels :]


def pack_rows(px, first, u_ref, p_ref, q_ref, wf_ref, mt_ref, got_ref, out):
    levels = out.shape[2]
    start = (1 - first) * (px - 2)
    for d in range(2):
        i = start + d
        out[0, d] = row(u_ref, i, levels, px)
        out[1, d] = row(p_ref, i, levels, px) * row(q_ref, i, levels, px)
        star = row(mt_ref, i, levels, px) + got_ref[pl.ds(((1 - first) * (2 * EDGE - 2) + d) * levels, levels), :]
        out[2, d] = row(wf_ref, i, levels, px) * star


def pack_even(px, u_ref, p_ref, q_ref, wf_ref, mt_ref, got_ref, e4_ref):
    odd4 = lax.rem(lax.div(lax.axis_index("cols"), TW), 2)
    pack_rows(px, odd4, u_ref, p_ref, q_ref, wf_ref, mt_ref, got_ref, e4_ref)


def pack(px, u_ref, v_ref, p_ref, q_ref, wf_ref, ws_ref, mt_ref, got_ref, o4_ref, e1_ref, o1_ref):
    levels = o4_ref.shape[2]
    py = o4_ref.shape[3]
    cols = lax.axis_index("cols")
    odd4 = lax.rem(lax.div(cols, TW), 2)
    odd1 = lax.rem(cols, 2)
    pack_rows(px, 1 - odd4, u_ref, p_ref, q_ref, wf_ref, mt_ref, got_ref, o4_ref)
    selector = rim_selector(py)
    got_rims = jnp.concatenate(
        [got_ref[pl.ds(2 * EDGE * levels + 4 * k, 4), :] for k in range(levels * px // py)], axis=1
    )
    v_rims = rims(v_ref[...], selector)[0:4]
    p_rims = rims(p_ref[...] * q_ref[...], selector)[0:4]
    t_rims = rims(ws_ref[...], selector)[0:4] * (rims(mt_ref[...], selector)[0:4] + got_rims)
    first = jnp.concatenate([v_rims[0:2], p_rims[0:2], t_rims[0:2]], axis=1)
    last = jnp.concatenate([v_rims[2:4], p_rims[2:4], t_rims[2:4]], axis=1)
    is_odd = odd1 == 1
    e1_ref[...] = jnp.where(is_odd, first, last)
    o1_ref[...] = jnp.where(is_odd, last, first)


def band(py):
    k = iota2((py, py), 0)
    j = iota2((py, py), 1)
    d = k - j
    one = jnp.where(d == 1, 8.0, jnp.where(d == -1, -8.0, 0.0))
    two = jnp.where(d == 2, -1.0, jnp.where(d == -2, 1.0, 0.0))
    return (one + two).astype(bf16)


def rim_band(py):
    k = iota2((4, py), 0)
    j = iota2((4, py), 1)
    d = jnp.where(k < 2, k - 2, py - 2 + k) - j
    one = jnp.where(d == 1, 8.0, jnp.where(d == -1, -8.0, 0.0))
    two = jnp.where(d == 2, -1.0, jnp.where(d == -2, 1.0, 0.0))
    return (one + two).astype(bf16)


def second_inner(field):
    center = band(field.shape[1])
    total = 0.0
    for piece in split(field):
        total = total + jnp.dot(piece, center, preferred_element_type=f32)
    return total * (1.0 / 12.0)


def second_rim(rim, py):
    edge = rim_band(py)
    total = 0.0
    for piece in split(rim):
        total = total + lax.dot_general(
            piece, edge, (((0,), (0,)), ((), ())), preferred_element_type=f32
        )
    return total * (1.0 / 12.0)


def first_inner(rows, i, px):
    one = rows(i + 1) if i + 1 < px else 0.0
    one = one - rows(i - 1) if i >= 1 else one
    two = rows(i + 2) if i + 2 < px else 0.0
    two = two - rows(i - 2) if i >= 2 else two
    return (8.0 * one - two) * (1.0 / 12.0)


def first_rim(i, before, after, px):
    if i == 0:
        return (before[0] - 8.0 * before[1]) * (1.0 / 12.0)
    if i == 1:
        return before[1] * (1.0 / 12.0)
    if i == px - 2:
        return after[0] * (-1.0 / 12.0)
    return (8.0 * after[0] - after[1]) * (1.0 / 12.0)


def first_inner(rows, i, px):
    one = rows(i + 1) if i + 1 < px else 0.0
    one = one - rows(i - 1) if i >= 1 else one
    two = rows(i + 2) if i + 2 < px else 0.0
    two = two - rows(i - 2) if i >= 2 else two
    return (8.0 * one - two) * (1.0 / 12.0)


def first_rim(i, before, after, px):
    if i == 0:
        return (before[0] - 8.0 * before[1]) * (1.0 / 12.0)
    if i == 1:
        return before[1] * (1.0 / 12.0)
    if i == px - 2:
        return after[0] * (-1.0 / 12.0)
    return (8.0 * after[0] - after[1]) * (1.0 / 12.0)


def winds_inner(px, u_ref, v_ref, p_ref, g_ref, q_ref, uo_ref, vo_ref, po_ref, pr_ref, gv_ref):
    levels = u_ref.shape[0] // px
    pressure = p_ref[...] * q_ref[...]
    pr_ref[...] = pressure
    vo_ref[...] = v_ref[...] + second_inner(pressure)
    gv_ref[...] = second_inner(v_ref[...])

    def u_rows(i):
        return row(u_ref, i, levels, px)

    def p_rows(i):
        return row(pr_ref, i, levels, px)

    for i in range(px):
        here = pl.ds(i, levels, stride=px)
        uo_ref[here, :] = u_ref[here, :] + first_inner(p_rows, i, px)
        po_ref[here, :] = p_ref[here, :] + g_ref[here, :] * (
            first_inner(u_rows, i, px) + gv_ref[here, :]
        )


def theta_inner(px, rim_ref, inner_ref, mt_ref, wf_ref, ws_ref, o_ref, star_ref, first_ref):
    levels = inner_ref.shape[1]
    for i in range(px):
        if EDGE <= i < px - EDGE:
            got = inner_ref[i - EDGE]
        else:
            got = rim_ref[pl.ds(rim_slot(i, px) * levels, levels), :]
        star = got + row(mt_ref, i, levels, px)
        star_ref[pl.ds(i, levels, stride=px), :] = star
        first_ref[i] = row(wf_ref, i, levels, px) * star
    star = star_ref[...]
    star_ref[...] = star + second_inner(ws_ref[...] * star)

    def rows(i):
        return first_ref[i]

    for i in range(px):
        here = pl.ds(i, levels, stride=px)
        o_ref[here, :] = star_ref[here, :] + first_inner(rows, i, px)


def halo_rows(e4_ref, o4_ref, at, odd):
    before = [jnp.where(odd, e4_ref[at, d], o4_ref[at, d]) for d in range(2)]
    after = [jnp.where(odd, o4_ref[at, d], e4_ref[at, d]) for d in range(2)]
    return before, after


def halo_columns(e1_ref, o1_ref, at, odd):
    cells = e1_ref.shape[1] // 3
    e1 = e1_ref[:, at * cells : (at + 1) * cells]
    o1 = o1_ref[:, at * cells : (at + 1) * cells]
    return jnp.concatenate([jnp.where(odd, e1, o1), jnp.where(odd, o1, e1)], axis=0)


def parities():
    cols = lax.axis_index("cols")
    return lax.rem(lax.div(cols, TW), 2) == 1, lax.rem(cols, 2) == 1


def finish(px, ub_ref, vb_ref, pb_ref, g_ref, tb_ref, e4_ref, o4_ref, e1_ref, o1_ref,
           u_hbm, v_hbm, t_hbm, p_hbm, u_ref, v_ref, t_ref, p_ref, sems):
    cells, py = ub_ref.shape
    levels = cells // px
    odd4, odd1 = parities()
    copies, send = sender(sems)
    edge_rows = (0, 1, px - 2, px - 1)
    u_ref[...] = ub_ref[...]
    before, after = halo_rows(e4_ref, o4_ref, 1, odd4)
    for i in edge_rows:
        here = pl.ds(i, levels, stride=px)
        u_ref[here, :] = ub_ref[here, :] + first_rim(i, before, after, px)
    send(u_ref, u_hbm)
    v_ref[...] = vb_ref[...] + second_rim(halo_columns(e1_ref, o1_ref, 1, odd1), py)
    send(v_ref, v_hbm)
    t_ref[...] = tb_ref[...] + second_rim(halo_columns(e1_ref, o1_ref, 2, odd1), py)
    before, after = halo_rows(e4_ref, o4_ref, 2, odd4)
    for i in edge_rows:
        here = pl.ds(i, levels, stride=px)
        t_ref[here, :] = t_ref[here, :] + first_rim(i, before, after, px)
    send(t_ref, t_hbm)
    p_ref[...] = pb_ref[...] + g_ref[...] * second_rim(halo_columns(e1_ref, o1_ref, 0, odd1), py)
    before, after = halo_rows(e4_ref, o4_ref, 0, odd4)
    for i in edge_rows:
        here = pl.ds(i, levels, stride=px)
        p_ref[here, :] = p_ref[here, :] + g_ref[here, :] * first_rim(i, before, after, px)
    send(p_ref, p_hbm)
    for copy in copies:
        copy.wait()


def kernel_for(px, body):
    def kernel(*refs):
        body(px, *refs)

    return kernel


def exchange(array, step, odd_pairs):
    devices = lax.axis_size("cols")
    pairs = []
    for c in range(devices):
        up = ((c // step) % 2 == 1) == odd_pairs
        pairs.append((c, (c + step if up else c - step) % devices))
    return lax.ppermute(array, "cols", pairs)


def on_device(u, v, w, t, p, grad, squeeze, wind_first, wind_second, a):
    levels, _, px, py = u.shape
    cells = levels * px
    u2, v2, w2, t2, p2, g2, q2, wf2, ws2 = (
        x.reshape(cells, py) for x in (u, v, w, t, p, grad, squeeze, wind_first, wind_second)
    )
    flat = (cells, py)
    rim_rows = 2 * EDGE * levels + 4 * (cells // py)
    rim_shape = (rim_rows, py)
    inner_shape = (px - 2 * EDGE, levels, py)
    rim_t, at = call(
        kernel_for(px, solve_first), "solve_first", [rim_shape, (4 * levels, 2 * levels)],
        [pltpu.VMEM((2, levels, px // 2, py), f32)] * 2
        + [pltpu.VMEM(a.shape, f32), pltpu.VMEM(flat, f32), pltpu.SemaphoreType.DMA((5,))],
        w.reshape(levels, px, py), t.reshape(levels, px, py), a, in_space=HBM, limit=FIRST_LIMIT, flops=LONG)
    (inner_t,) = call(
        kernel_for(px, solve_inner), "solve_inner", [inner_shape], [], w2, t2, at, flops=I_COST)
    got_rim = passed_along(rim_t, "lev", 1)
    got_inner = passed_along(inner_t, "lev", 1)
    other_w, mine_w, mine_t = call(
        kernel_for(px, solve_rest), "solve_rest", [flat] * 3, [], w2, t2, at, flops=LONG, after=(inner_t,))
    o4, e1, o1 = call(
        kernel_for(px, pack), "pack", [(3, 2, levels, py)] + [(2, 3 * cells)] * 2, [],
        u2, v2, p2, q2, wf2, ws2, mine_t, got_rim, flops=LONG, after=(other_w,))
    (e4,) = call(
        kernel_for(px, pack_even), "pack_even", [(3, 2, levels, py)], [],
        u2, p2, q2, wf2, mine_t, got_rim, flops=LONG, after=(o1,))
    got_w = passed_along(other_w, "lev", 1)
    halos = (exchange(e4, TW, False), exchange(o4, TW, True), exchange(e1, 1, False), exchange(o1, 1, True))
    u_in, v_in, p_in = call(
        kernel_for(px, winds_inner), "winds_inner", [flat] * 3, [pltpu.VMEM(flat, f32)] * 2,
        u2, v2, p2, g2, q2, after=(e4,), flops=W_COST)
    (t_in,) = call(
        kernel_for(px, theta_inner), "theta_inner", [flat],
        [pltpu.VMEM(flat, f32), pltpu.VMEM((px, levels, py), f32)],
        got_rim, got_inner, mine_t, wf2, ws2, flops=T_COST)
    w_out = mine_w + got_w
    u_out, v_out, theta_out, p_out = call(
        kernel_for(px, finish), "finish", [flat] * 4,
        [pltpu.VMEM(flat, f32)] * 4 + [pltpu.SemaphoreType.DMA((4,))],
        u_in, v_in, p_in, g2, t_in, *halos, out_space=HBM, flops=F_COST)
    outs = (u_out, v_out, w_out, theta_out, p_out)
    return tuple(x.reshape(u.shape) for x in outs)


def solution(mesh):
    spread = P("lev", "cols", None, None)
    return jax.shard_map(
        on_device,
        mesh=mesh,
        in_specs=(spread,) * 9 + (P(),),
        out_specs=(spread,) * 5,
        check_vma=False,
    )
```

```python
import jax
import jax.numpy as jnp
from jax import lax
from jax.experimental import pallas as pl
from jax.experimental.pallas import tpu as pltpu
from jax.sharding import PartitionSpec as P

TW = 4
EDGE = 3
FIRST_LIMIT = (53 << 20) + (560 << 10)
LONG = 12_000_000_000
W_COST = 0
I_COST = 0
T_COST = 0
F_COST = 0
f32 = jnp.float32
bf16 = jnp.bfloat16
VMEM = pl.BlockSpec(memory_space=pltpu.VMEM)


def passed_along(array, axis, by):
    devices = lax.axis_size(axis)
    return lax.ppermute(array, axis, [(i, (i + by) % devices) for i in range(devices)])


def split(x):
    high = x.astype(bf16)
    return high, (x - high.astype(f32)).astype(bf16)


def split3(x):
    high = x.astype(bf16)
    rest = x - high.astype(f32)
    middle = rest.astype(bf16)
    return high, middle, (rest - middle.astype(f32)).astype(bf16)


HBM = pl.BlockSpec(memory_space=pl.ANY)


def call(kernel, name, outs, scratch, *args, flops=0, in_space=VMEM, out_space=VMEM, limit=32 << 20, after=()):
    shapes = tuple(jax.ShapeDtypeStruct(s, f32) for s in outs)
    size = sum(a.size for a in args) + sum(s.size for s in shapes)

    def body(*refs):
        kernel(*refs[: len(args)], *refs[len(args) + len(after) :])

    return pl.pallas_call(
        body,
        out_shape=shapes,
        in_specs=[in_space] * len(args) + [HBM] * len(after),
        out_specs=out_space if isinstance(out_space, tuple) else (out_space,) * len(shapes),
        scratch_shapes=scratch,
        name=name,
        cost_estimate=pl.CostEstimate(flops=flops, bytes_accessed=4 * size, transcendentals=0),
        compiler_params=pltpu.CompilerParams(vmem_limit_bytes=limit),
    )(*args, *after)


def row(ref, i, levels, px):
    return ref[pl.ds(i, levels, stride=px), :]


def left_factor(blocks):
    high, low = split(jnp.concatenate(blocks, axis=0))
    return jnp.concatenate(
        [jnp.concatenate([high, high], axis=1), jnp.concatenate([low, low], axis=1)], axis=0
    )


def paired(pieces):
    halves = []
    for w_part, t_part in pieces:
        halves.append(jnp.concatenate(split(jnp.concatenate([w_part, t_part], axis=0)), axis=0))
    return jnp.concatenate(halves, axis=1)


def iota2(shape, dim):
    return lax.broadcasted_iota(jnp.int32, shape, dim)


def rim_selector(py):
    k = iota2((8, py), 0)
    j = iota2((8, py), 1)
    want = jnp.where(k < 2, k, py - 4 + k)
    return jnp.where((j == want) & (k < 4), 1.0, 0.0).astype(bf16)


def rims(field, selector, parts=split3):
    total = 0.0
    for piece in parts(field):
        total = total + lax.dot_general(
            selector, piece, (((1,), (1,)), ((), ())), preferred_element_type=f32
        )
    return total


def rim_slot(i, px):
    return i if i < EDGE else i - px + 2 * EDGE


def sender(sems):
    copies = []

    def send(source, target):
        copy = pltpu.make_async_copy(source, target, sems.at[len(copies)])
        copy.start()
        copies.append(copy)

    return copies, send


def solve_first(px, w_hbm, t_hbm, a_hbm, rim_ref, at_ref, w_ref, t_ref, a_ref, full_ref, sems):
    levels, _, py = w_hbm.shape
    half = px // 2
    copies, send = sender(sems)
    send(a_hbm, a_ref)
    for h in range(2):
        here = pl.ds(h * half, half)
        send(w_hbm.at[:, here, :], w_ref.at[h])
        send(t_hbm.at[:, here, :], t_ref.at[h])
    me = lax.axis_index("lev")
    copies[0].wait()
    rows = jnp.concatenate(
        [a_ref[pl.ds(me * levels, levels), :], a_ref[pl.ds((2 + me) * levels, levels), :]], axis=0
    )
    at_ref[...] = rows.T
    left = left_factor([at_ref[pl.ds((3 - me) * levels, levels), :]])
    for h in range(2):
        copies[1 + 2 * h].wait()
        copies[2 + 2 * h].wait()
        w_half = w_ref.at[h].reshape(levels * half, py)
        t_half = t_ref.at[h].reshape(levels * half, py)
        for k, part in solved(half, left, w_half, t_half):
            i = h * half + k
            full_ref[pl.ds(i, levels, stride=px), :] = part
            if not EDGE <= i < px - EDGE:
                rim_ref[pl.ds(rim_slot(i, px) * levels, levels), :] = part
    edges = rims(full_ref[...], rim_selector(py), split)
    for k in range(levels * px // py):
        rim_ref[pl.ds(2 * EDGE * levels + 4 * k, 4), :] = edges[0:4, k * py : (k + 1) * py]


def solved(px, left, w_ref, t_ref, skip=0):
    levels = w_ref.shape[0] // px
    py = w_ref.shape[1]
    half = left.shape[0] // 2
    for i in range(skip, px - skip, 2):
        right = paired([(row(w_ref, i + d, levels, px), row(t_ref, i + d, levels, px)) for d in range(2)])
        r = jnp.dot(left, right, preferred_element_type=f32)
        r = r[:half] + r[half:]
        yield i, r[:, :py]
        yield i + 1, r[:, py:]


def solve_inner(px, w_ref, t_ref, at_ref, inner_ref):
    levels = w_ref.shape[0] // px
    me = lax.axis_index("lev")
    left = left_factor([at_ref[pl.ds((3 - me) * levels, levels), :]])
    for i, part in solved(px, left, w_ref, t_ref, EDGE // 2 * 2):
        if EDGE <= i < px - EDGE:
            inner_ref[i - EDGE] = part


def solve_rest(px, w_ref, t_ref, at_ref, ow_ref, mw_ref, mt_ref):
    levels = w_ref.shape[0] // px
    me = lax.axis_index("lev")
    left = left_factor(
        [
            at_ref[pl.ds((1 - me) * levels, levels), :],
            at_ref[pl.ds(me * levels, levels), :],
            at_ref[pl.ds((2 + me) * levels, levels), :],
        ]
    )
    for i, part in solved(px, left, w_ref, t_ref):
        here = pl.ds(i, levels, stride=px)
        ow_ref[here, :] = part[:levels]
        mw_ref[here, :] = part[levels : 2 * levels]
        mt_ref[here, :] = part[2 * levels :]


def pack_rows(px, first, u_ref, p_ref, q_ref, wf_ref, mt_ref, got_ref, out):
    levels = out.shape[2]
    start = (1 - first) * (px - 2)
    for d in range(2):
        i = start + d
        out[0, d] = row(u_ref, i, levels, px)
        out[1, d] = row(p_ref, i, levels, px) * row(q_ref, i, levels, px)
        star = row(mt_ref, i, levels, px) + got_ref[pl.ds(((1 - first) * (2 * EDGE - 2) + d) * levels, levels), :]
        out[2, d] = row(wf_ref, i, levels, px) * star


def pack_even(px, u_ref, p_ref, q_ref, wf_ref, mt_ref, got_ref, e4_ref):
    odd4 = lax.rem(lax.div(lax.axis_index("cols"), TW), 2)
    pack_rows(px, odd4, u_ref, p_ref, q_ref, wf_ref, mt_ref, got_ref, e4_ref)


def pack(px, u_ref, v_ref, p_ref, q_ref, wf_ref, ws_ref, mt_ref, got_ref, o4_ref, e1_ref, o1_ref):
    levels = o4_ref.shape[2]
    py = o4_ref.shape[3]
    cols = lax.axis_index("cols")
    odd4 = lax.rem(lax.div(cols, TW), 2)
    odd1 = lax.rem(cols, 2)
    pack_rows(px, 1 - odd4, u_ref, p_ref, q_ref, wf_ref, mt_ref, got_ref, o4_ref)
    selector = rim_selector(py)
    got_rims = jnp.concatenate(
        [got_ref[pl.ds(2 * EDGE * levels + 4 * k, 4), :] for k in range(levels * px // py)], axis=1
    )
    v_rims = rims(v_ref[...], selector)[0:4]
    p_rims = rims(p_ref[...] * q_ref[...], selector)[0:4]
    t_rims = rims(ws_ref[...], selector)[0:4] * (rims(mt_ref[...], selector)[0:4] + got_rims)
    first = jnp.concatenate([v_rims[0:2], p_rims[0:2], t_rims[0:2]], axis=1)
    last = jnp.concatenate([v_rims[2:4], p_rims[2:4], t_rims[2:4]], axis=1)
    is_odd = odd1 == 1
    e1_ref[...] = jnp.where(is_odd, first, last)
    o1_ref[...] = jnp.where(is_odd, last, first)


def band(py):
    k = iota2((py, py), 0)
    j = iota2((py, py), 1)
    d = k - j
    one = jnp.where(d == 1, 8.0, jnp.where(d == -1, -8.0, 0.0))
    two = jnp.where(d == 2, -1.0, jnp.where(d == -2, 1.0, 0.0))
    return (one + two).astype(bf16)


def rim_band(py):
    k = iota2((4, py), 0)
    j = iota2((4, py), 1)
    d = jnp.where(k < 2, k - 2, py - 2 + k) - j
    one = jnp.where(d == 1, 8.0, jnp.where(d == -1, -8.0, 0.0))
    two = jnp.where(d == 2, -1.0, jnp.where(d == -2, 1.0, 0.0))
    return (one + two).astype(bf16)


def second_inner(field):
    center = band(field.shape[1])
    total = 0.0
    for piece in split(field):
        total = total + jnp.dot(piece, center, preferred_element_type=f32)
    return total * (1.0 / 12.0)


def second_rim(rim, py):
    edge = rim_band(py)
    total = 0.0
    for piece in split(rim):
        total = total + lax.dot_general(
            piece, edge, (((0,), (0,)), ((), ())), preferred_element_type=f32
        )
    return total * (1.0 / 12.0)


def first_inner(rows, i, px):
    one = rows(i + 1) if i + 1 < px else 0.0
    one = one - rows(i - 1) if i >= 1 else one
    two = rows(i + 2) if i + 2 < px else 0.0
    two = two - rows(i - 2) if i >= 2 else two
    return (8.0 * one - two) * (1.0 / 12.0)


def first_rim(i, before, after, px):
    if i == 0:
        return (before[0] - 8.0 * before[1]) * (1.0 / 12.0)
    if i == 1:
        return before[1] * (1.0 / 12.0)
    if i == px - 2:
        return after[0] * (-1.0 / 12.0)
    return (8.0 * after[0] - after[1]) * (1.0 / 12.0)


def first_inner(rows, i, px):
    one = rows(i + 1) if i + 1 < px else 0.0
    one = one - rows(i - 1) if i >= 1 else one
    two = rows(i + 2) if i + 2 < px else 0.0
    two = two - rows(i - 2) if i >= 2 else two
    return (8.0 * one - two) * (1.0 / 12.0)


def first_rim(i, before, after, px):
    if i == 0:
        return (before[0] - 8.0 * before[1]) * (1.0 / 12.0)
    if i == 1:
        return before[1] * (1.0 / 12.0)
    if i == px - 2:
        return after[0] * (-1.0 / 12.0)
    return (8.0 * after[0] - after[1]) * (1.0 / 12.0)


def winds_inner(px, u_ref, v_ref, p_ref, g_ref, q_ref, uo_ref, vo_ref, po_ref, pr_ref, gv_ref):
    levels = u_ref.shape[0] // px
    pressure = p_ref[...] * q_ref[...]
    pr_ref[...] = pressure
    vo_ref[...] = v_ref[...] + second_inner(pressure)
    gv_ref[...] = second_inner(v_ref[...])

    def u_rows(i):
        return row(u_ref, i, levels, px)

    def p_rows(i):
        return row(pr_ref, i, levels, px)

    for i in range(px):
        here = pl.ds(i, levels, stride=px)
        uo_ref[here, :] = u_ref[here, :] + first_inner(p_rows, i, px)
        po_ref[here, :] = p_ref[here, :] + g_ref[here, :] * (
            first_inner(u_rows, i, px) + gv_ref[here, :]
        )


def theta_inner(px, rim_ref, inner_ref, mt_ref, wf_ref, ws_ref, o_ref, star_ref, first_ref):
    levels = inner_ref.shape[1]
    for i in range(px):
        if EDGE <= i < px - EDGE:
            got = inner_ref[i - EDGE]
        else:
            got = rim_ref[pl.ds(rim_slot(i, px) * levels, levels), :]
        star = got + row(mt_ref, i, levels, px)
        star_ref[pl.ds(i, levels, stride=px), :] = star
        first_ref[i] = row(wf_ref, i, levels, px) * star
    star = star_ref[...]
    star_ref[...] = star + second_inner(ws_ref[...] * star)

    def rows(i):
        return first_ref[i]

    for i in range(px):
        here = pl.ds(i, levels, stride=px)
        o_ref[here, :] = star_ref[here, :] + first_inner(rows, i, px)


def halo_rows(e4_ref, o4_ref, at, odd):
    before = [jnp.where(odd, e4_ref[at, d], o4_ref[at, d]) for d in range(2)]
    after = [jnp.where(odd, o4_ref[at, d], e4_ref[at, d]) for d in range(2)]
    return before, after


def halo_columns(e1_ref, o1_ref, at, odd):
    cells = e1_ref.shape[1] // 3
    e1 = e1_ref[:, at * cells : (at + 1) * cells]
    o1 = o1_ref[:, at * cells : (at + 1) * cells]
    return jnp.concatenate([jnp.where(odd, e1, o1), jnp.where(odd, o1, e1)], axis=0)


def parities():
    cols = lax.axis_index("cols")
    return lax.rem(lax.div(cols, TW), 2) == 1, lax.rem(cols, 2) == 1


def finish(px, ub_ref, vb_ref, pb_ref, g_ref, tb_ref, e4_ref, o4_ref, e1_ref, o1_ref,
           u_hbm, v_hbm, t_hbm, p_hbm, u_ref, v_ref, t_ref, p_ref, sems):
    cells, py = ub_ref.shape
    levels = cells // px
    odd4, odd1 = parities()
    copies, send = sender(sems)
    edge_rows = (0, 1, px - 2, px - 1)
    u_ref[...] = ub_ref[...]
    before, after = halo_rows(e4_ref, o4_ref, 1, odd4)
    for i in edge_rows:
        here = pl.ds(i, levels, stride=px)
        u_ref[here, :] = ub_ref[here, :] + first_rim(i, before, after, px)
    send(u_ref, u_hbm)
    v_ref[...] = vb_ref[...] + second_rim(halo_columns(e1_ref, o1_ref, 1, odd1), py)
    send(v_ref, v_hbm)
    t_ref[...] = tb_ref[...] + second_rim(halo_columns(e1_ref, o1_ref, 2, odd1), py)
    before, after = halo_rows(e4_ref, o4_ref, 2, odd4)
    for i in edge_rows:
        here = pl.ds(i, levels, stride=px)
        t_ref[here, :] = t_ref[here, :] + first_rim(i, before, after, px)
    send(t_ref, t_hbm)
    p_ref[...] = pb_ref[...] + g_ref[...] * second_rim(halo_columns(e1_ref, o1_ref, 0, odd1), py)
    before, after = halo_rows(e4_ref, o4_ref, 0, odd4)
    for i in edge_rows:
        here = pl.ds(i, levels, stride=px)
        p_ref[here, :] = p_ref[here, :] + g_ref[here, :] * first_rim(i, before, after, px)
    send(p_ref, p_hbm)
    for copy in copies:
        copy.wait()


def kernel_for(px, body):
    def kernel(*refs):
        body(px, *refs)

    return kernel


def exchange(array, step, odd_pairs):
    devices = lax.axis_size("cols")
    pairs = []
    for c in range(devices):
        up = ((c // step) % 2 == 1) == odd_pairs
        pairs.append((c, (c + step if up else c - step) % devices))
    return lax.ppermute(array, "cols", pairs)


def on_device(u, v, w, t, p, grad, squeeze, wind_first, wind_second, a):
    levels, _, px, py = u.shape
    cells = levels * px
    u2, v2, w2, t2, p2, g2, q2, wf2, ws2 = (
        x.reshape(cells, py) for x in (u, v, w, t, p, grad, squeeze, wind_first, wind_second)
    )
    flat = (cells, py)
    rim_rows = 2 * EDGE * levels + 4 * (cells // py)
    rim_shape = (rim_rows, py)
    inner_shape = (px - 2 * EDGE, levels, py)
    rim_t, at = call(
        kernel_for(px, solve_first), "solve_first", [rim_shape, (4 * levels, 2 * levels)],
        [pltpu.VMEM((2, levels, px // 2, py), f32)] * 2
        + [pltpu.VMEM(a.shape, f32), pltpu.VMEM(flat, f32), pltpu.SemaphoreType.DMA((5,))],
        w.reshape(levels, px, py), t.reshape(levels, px, py), a, in_space=HBM, limit=FIRST_LIMIT, flops=LONG)
    (inner_t,) = call(
        kernel_for(px, solve_inner), "solve_inner", [inner_shape], [], w2, t2, at, flops=I_COST)
    got_rim = passed_along(rim_t, "lev", 1)
    got_inner = passed_along(inner_t, "lev", 1)
    other_w, mine_w, mine_t = call(
        kernel_for(px, solve_rest), "solve_rest", [flat] * 3, [], w2, t2, at, flops=LONG, after=(inner_t,))
    o4, e1, o1 = call(
        kernel_for(px, pack), "pack", [(3, 2, levels, py)] + [(2, 3 * cells)] * 2, [],
        u2, v2, p2, q2, wf2, ws2, mine_t, got_rim, flops=LONG, after=(other_w,))
    (e4,) = call(
        kernel_for(px, pack_even), "pack_even", [(3, 2, levels, py)], [],
        u2, p2, q2, wf2, mine_t, got_rim, flops=LONG, after=(o1,))
    got_w = passed_along(other_w, "lev", 1)
    halos = (exchange(e4, TW, False), exchange(o4, TW, True), exchange(e1, 1, False), exchange(o1, 1, True))
    u_in, v_in, p_in = call(
        kernel_for(px, winds_inner), "winds_inner", [flat] * 3, [pltpu.VMEM(flat, f32)] * 2,
        u2, v2, p2, g2, q2, after=(e4,), flops=W_COST)
    (t_in,) = call(
        kernel_for(px, theta_inner), "theta_inner", [flat],
        [pltpu.VMEM(flat, f32), pltpu.VMEM((px, levels, py), f32)],
        got_rim, got_inner, mine_t, wf2, ws2, flops=T_COST)
    w_out = mine_w + got_w
    u_out, v_out, theta_out, p_out = call(
        kernel_for(px, finish), "finish", [flat] * 4,
        [pltpu.VMEM(flat, f32)] * 4 + [pltpu.SemaphoreType.DMA((4,))],
        u_in, v_in, p_in, g2, t_in, *halos, out_space=HBM, flops=F_COST)
    outs = (u_out, v_out, w_out, theta_out, p_out)
    return tuple(x.reshape(u.shape) for x in outs)


def solution(mesh):
    spread = P("lev", "cols", None, None)
    return jax.shard_map(
        on_device,
        mesh=mesh,
        in_specs=(spread,) * 9 + (P(),),
        out_specs=(spread,) * 5,
        check_vma=False,
    )
```
